32 devices in a mesh: ens: 2 (over y), lat: 16 (over z, x, core).
Axes of the slice: x: 2, y: 2, z: 4, core: 2. Of those that a mesh axis runs over, the one named last changes fastest.
Arguments:
- field: bfloat16 [2, 48, 96, 256], P('ens', 'lat'), parts along dimension 0, may hold values from -6 to 6
- filters: bfloat16 [2, 48, 256], replicated, may hold values from -5 to 5
- weight_in: bfloat16 [256, 512], replicated, may hold values from -0.375 to 0.375
- weight_out: bfloat16 [512, 256], replicated, may hold values from -0.25 to 0.25
- norm_gain: float32 [256], replicated, may hold values from 0.5 to 1.5
- cotangent: bfloat16 [2, 48, 96, 256], P('ens', 'lat'), parts along dimension 0, may hold values from -6 to 6
Outputs:
- block_out: bfloat16 [2, 48, 96, 256], P('ens', 'lat'), parts along dimension 0
- grad_field: bfloat16 [2, 48, 96, 256], P('ens', 'lat'), parts along dimension 0
- grad_filters: float32 [4, 48, 256], P('ens'), parts along dimension 0
- grad_weight_in: float32 [512, 512], P('ens'), parts along dimension 0
- grad_weight_out: float32 [1024, 256], P('ens'), parts along dimension 0
- grad_gain: float32 [512], P('ens'), parts along dimension 0
The draws below stay inside these ranges and needn't reach their ends.
There are 2 independent parts, one for each index of `ens`. The reference program is written for one: setup_inputs(seed, part) draws one part's arguments, and reference() takes and returns one part's arrays. A program takes and returns all parts, laid end to end along the dimension named above; an argument that names none is the same for every part. Nothing has to cross between parts.
All inputs are finite; a program needn't handle non-finite values.
Results may differ from the reference program's by a relative error of at most 0.018.
Values may be sent and summed in bfloat16 or wider, within the bound.
A program may use at most 128 MiB of HBM per device.

```python
import math
import jax
import jax.numpy as jnp
from jax import lax

E = 256
HID = 512
MEM = 1
NLAT = 48
NLON = 96


def steps_of(key, shape, split, smallest, high):
    factor_of, own = 1.0, jax.random.fold_in(key, 6)
    for position, parts in split:
        heights = jnp.exp(jax.random.uniform(jax.random.fold_in(own, position), (parts,), jnp.float32, smallest / len(split), high / len(split)))
        factor_of = factor_of * jnp.repeat(heights, shape[position] // parts).reshape([-1 if axis == position else 1 for axis in range(len(shape))])
    return factor_of


def scatter_about(stream_key, extent, scale, reach, pieces=(), kind=jnp.bfloat16):
    drawn = jax.random.normal(stream_key, extent, jnp.float32) * scale
    if len(pieces) > 0:
        drawn = steps_of(stream_key, extent, pieces, -0.22, 0.18) * drawn
    return jnp.clip(drawn, min=-reach, max=reach).astype(kind)


def setup_inputs(seed: int = 0, part: int = 0) -> dict:
    arg_keys = jax.random.split(jax.random.key(seed), 7)
    own_keys = jax.random.split(jax.random.fold_in(arg_keys[6], part), 7)
    field = scatter_about(own_keys[0], (MEM, NLAT, NLON, E), 1.0, 6.0, ((1, 16),))
    filters = scatter_about(arg_keys[1], (2, NLAT, E), 1.0, 5.0)
    weight_in = scatter_about(arg_keys[2], (E, HID), E ** -0.5, 0.375)
    weight_out = scatter_about(arg_keys[3], (HID, E), HID ** -0.5, 0.25)
    norm_gain = jnp.clip(1.0 + 0.1 * jax.random.normal(arg_keys[4], (E,), jnp.float32), 0.5, 1.5)
    cotangent = scatter_about(own_keys[5], (MEM, NLAT, NLON, E), 1.0, 6.0, ((1, 16),))
    return dict(field=field, filters=filters, weight_in=weight_in, weight_out=weight_out, norm_gain=norm_gain, cotangent=cotangent)


EPSILON = 1e-05

def compose_maps(earlier, later):
    e00, e01, e10, e11, ec0, ec1 = earlier
    l00, l01, l10, l11, lc0, lc1 = later
    return (l00 * e00 + l01 * e10, l00 * e01 + l01 * e11, l10 * e00 + l11 * e10, l10 * e01 + l11 * e11, l00 * ec0 + l01 * ec1 + lc0, l10 * ec0 + l11 * ec1 + lc1)

def legendre(lat_total, orders, degree_count):
    colatitude = (jnp.arange(lat_total, dtype=jnp.float32) + 0.5) * (math.pi / lat_total)
    cosine = jnp.cos(colatitude)[None, :, None]
    sine_theta = jnp.sin(colatitude)[:, None]
    morder_row = orders.astype(jnp.float32)[None, :]
    log_start = 0.5 * (jnp.log((2.0 * morder_row + 1.0) / (4.0 * math.pi)) + lax.lgamma(morder_row + 0.5) - lax.lgamma(morder_row + 1.0) - 0.5 * math.log(math.pi)) + morder_row * jnp.log(sine_theta)
    diagonal = jnp.exp(log_start)[None, :, :]
    morder = orders.astype(jnp.float32)[None, None, :]
    order_rows = orders[None, None, :]
    degree = jnp.arange(degree_count, dtype=jnp.int32)[:, None, None]
    degree_f = degree.astype(jnp.float32)
    ratio_a = jnp.sqrt((4.0 * degree_f * degree_f - 1.0) / jnp.maximum(degree_f * degree_f - morder * morder, 1.0))
    previous_f = degree_f - 1.0
    ratio_b = jnp.sqrt(jnp.maximum(previous_f * previous_f - morder * morder, 0.0) / jnp.maximum(4.0 * previous_f * previous_f - 1.0, 1.0))
    shape = (degree_count, lat_total, orders.shape[0])
    general = degree >= order_rows + 2
    step_one = degree == order_rows + 1
    at_start = degree == order_rows
    zero_map = jnp.zeros(shape, jnp.float32)
    first_row = jnp.where(general, ratio_a * cosine, jnp.where(step_one, jnp.sqrt(2.0 * morder + 3.0) * cosine, 0.0))
    second_entry = jnp.where(general, -ratio_a * ratio_b, 0.0) + zero_map
    lower_entry = jnp.where(degree > order_rows, 1.0, 0.0) + zero_map
    offset = jnp.where(at_start, diagonal, 0.0) + zero_map
    elements = (first_row + zero_map, second_entry, lower_entry, zero_map, offset, zero_map)
    composed = lax.associative_scan(compose_maps, elements, axis=0)
    return jnp.transpose(composed[4], (1, 2, 0))

def legendre_all(lat_total, degree_count):

    def one_order(order_value):
        return legendre(lat_total, order_value[None], degree_count)[:, 0, :]
    stacked = lax.map(one_order, jnp.arange(degree_count, dtype=jnp.int32))
    return jnp.transpose(stacked, (1, 0, 2))

def latitude_weights(lat_total):
    colatitude = (jnp.arange(lat_total, dtype=jnp.float32) + 0.5) * (math.pi / lat_total)
    return jnp.sin(colatitude) * (math.pi / lat_total)

def forward_table(lon_cells, order_count):
    lon_index = jnp.arange(lon_cells, dtype=jnp.int32)[:, None]
    order_index = jnp.arange(order_count, dtype=jnp.int32)[None, :]
    angles = (lon_index * order_index % lon_cells).astype(jnp.float32) * (2.0 * math.pi / lon_cells)
    factor = 2.0 * math.pi / lon_cells
    return jnp.concatenate([jnp.cos(angles) * factor, -jnp.sin(angles) * factor], axis=1).astype(jnp.bfloat16)

def inverse_table(lon_cells, order_count):
    order_index = jnp.arange(order_count, dtype=jnp.int32)[:, None]
    lon_index = jnp.arange(lon_cells, dtype=jnp.int32)[None, :]
    angles = (lon_index * order_index % lon_cells).astype(jnp.float32) * (2.0 * math.pi / lon_cells)
    factor = jnp.where(order_index == 0, 1.0, 2.0)
    return jnp.concatenate([factor * jnp.cos(angles), -factor * jnp.sin(angles)], axis=0).astype(jnp.bfloat16)

def gelu_slope(preact):
    return 0.5 * (1.0 + lax.erf(preact * 0.7071067811865476)) + preact * jnp.exp(-0.5 * preact * preact) * 0.3989422804014327

def rounded(value):
    return lax.optimization_barrier(value.astype(jnp.bfloat16)).astype(jnp.float32)

def reference(field, filters, weight_in, weight_out, norm_gain, cotangent):
    members, lat_rows, lon_cells, channels = field.shape
    degrees = lat_rows
    forward = forward_table(lon_cells, degrees).astype(jnp.float32)
    inverse = inverse_table(lon_cells, degrees).astype(jnp.float32)
    legendre_table = legendre_all(lat_rows, degrees)
    synth_table = rounded(legendre_table)
    analysis_table = rounded(latitude_weights(lat_rows)[:, None, None] * legendre_table)
    spectral = rounded(jnp.einsum('bjkc,kn->bjnc', field.astype(jnp.float32), forward))
    spectral = spectral.reshape(members, lat_rows, 2, degrees, channels)
    coeffs = rounded(jnp.einsum('jml,bjrmc->brmlc', analysis_table, spectral))
    spectral_gain = filters.astype(jnp.float32)
    real_part = coeffs[:, 0] * spectral_gain[0] - coeffs[:, 1] * spectral_gain[1]
    imag_part = coeffs[:, 0] * spectral_gain[1] + coeffs[:, 1] * spectral_gain[0]
    filtered = rounded(jnp.stack([real_part, imag_part], axis=1))
    synthesized = rounded(jnp.einsum('jml,brmlc->bjrmc', synth_table, filtered))
    back = jnp.einsum('bjnc,nk->bjkc', synthesized.reshape(members, lat_rows, 2 * degrees, channels), inverse)
    summed = rounded(field.astype(jnp.float32) + back)
    average = lax.optimization_barrier(jnp.mean(summed, axis=-1, keepdims=True))
    centered = summed - average
    inverse_std = lax.rsqrt(lax.optimization_barrier(jnp.mean(centered * centered, axis=-1, keepdims=True)) + EPSILON)
    normal = centered * inverse_std
    normed = rounded(normal * norm_gain)
    preact = jnp.einsum('bjkc,ch->bjkh', normed, weight_in.astype(jnp.float32))
    hidden = rounded(jax.nn.gelu(preact, approximate=False))
    block_out = (summed + jnp.einsum('bjkh,hc->bjkc', hidden, weight_out.astype(jnp.float32))).astype(jnp.bfloat16)
    upstream = cotangent.astype(jnp.float32)
    grad_pre = rounded(jnp.einsum('bjkc,hc->bjkh', upstream, weight_out.astype(jnp.float32)) * gelu_slope(preact))
    grad_normed = jnp.einsum('bjkh,ch->bjkc', grad_pre, weight_in.astype(jnp.float32))
    grad_normal = grad_normed * norm_gain
    grad_summed = upstream + inverse_std * (grad_normal - lax.optimization_barrier(jnp.mean(grad_normal, axis=-1, keepdims=True)) - normal * lax.optimization_barrier(jnp.mean(grad_normal * normal, axis=-1, keepdims=True)))
    grad_rounded = rounded(grad_summed)
    grad_synth = rounded(jnp.einsum('bjkc,nk->bjnc', grad_rounded, inverse)).reshape(members, lat_rows, 2, degrees, channels)
    grad_filtered = jnp.einsum('jml,bjrmc->brmlc', synth_table, grad_synth)
    grad_real = grad_filtered[:, 0]
    grad_imag = grad_filtered[:, 1]
    grad_scale = 1.0 / math.sqrt(members * lat_rows * lon_cells)
    filter_real = lax.optimization_barrier(jnp.sum(coeffs[:, 0] * grad_real + coeffs[:, 1] * grad_imag, axis=(0, 1)))
    filter_imag = lax.optimization_barrier(jnp.sum(coeffs[:, 0] * grad_imag - coeffs[:, 1] * grad_real, axis=(0, 1)))
    grad_filters = jnp.stack([filter_real, filter_imag], axis=0) * grad_scale
    coeff_real = grad_real * spectral_gain[0] + grad_imag * spectral_gain[1]
    coeff_imag = grad_imag * spectral_gain[0] - grad_real * spectral_gain[1]
    grad_coeffs = rounded(jnp.stack([coeff_real, coeff_imag], axis=1))
    grad_spectral = rounded(jnp.einsum('jml,brmlc->bjrmc', analysis_table, grad_coeffs))
    grad_field = (grad_summed + jnp.einsum('bjnc,kn->bjkc', grad_spectral.reshape(members, lat_rows, 2 * degrees, channels), forward)).astype(jnp.bfloat16)
    grad_weight_in = jnp.einsum('bjkc,bjkh->ch', normed, grad_pre) * grad_scale
    grad_weight_out = jnp.einsum('bjkh,bjkc->hc', hidden, upstream) * grad_scale
    grad_gain = lax.optimization_barrier(jnp.sum(grad_normed * normal, axis=(0, 1, 2))) * grad_scale
    return (block_out, grad_field, grad_filters, grad_weight_in, grad_weight_out, grad_gain)
```

```python
import functools
import math

import jax
import jax.numpy as jnp
import ml_dtypes
import numpy as np
from jax import lax
from jax.experimental import pallas as pl
from jax.experimental.pallas import tpu as pltpu
from jax.sharding import PartitionSpec as P

EPSILON = 1e-05


def compose_maps(earlier, later):
    e00, e01, e10, e11, ec0, ec1 = earlier
    l00, l01, l10, l11, lc0, lc1 = later
    return (
        l00 * e00 + l01 * e10,
        l00 * e01 + l01 * e11,
        l10 * e00 + l11 * e10,
        l10 * e01 + l11 * e11,
        l00 * ec0 + l01 * ec1 + lc0,
        l10 * ec0 + l11 * ec1 + lc1,
    )


def legendre(lat_total, orders, degree_count):
    colatitude = (jnp.arange(lat_total, dtype=jnp.float32) + 0.5) * (math.pi / lat_total)
    cosine = jnp.cos(colatitude)[None, :, None]
    sine_theta = jnp.sin(colatitude)[:, None]
    morder_row = orders.astype(jnp.float32)[None, :]
    log_start = 0.5 * (
        jnp.log((2.0 * morder_row + 1.0) / (4.0 * math.pi))
        + lax.lgamma(morder_row + 0.5)
        - lax.lgamma(morder_row + 1.0)
        - 0.5 * math.log(math.pi)
    ) + morder_row * jnp.log(sine_theta)
    diagonal = jnp.exp(log_start)[None, :, :]
    morder = orders.astype(jnp.float32)[None, None, :]
    order_rows = orders[None, None, :]
    degree = jnp.arange(degree_count, dtype=jnp.int32)[:, None, None]
    degree_f = degree.astype(jnp.float32)
    ratio_a = jnp.sqrt(
        (4.0 * degree_f * degree_f - 1.0) / jnp.maximum(degree_f * degree_f - morder * morder, 1.0)
    )
    previous_f = degree_f - 1.0
    ratio_b = jnp.sqrt(
        jnp.maximum(previous_f * previous_f - morder * morder, 0.0)
        / jnp.maximum(4.0 * previous_f * previous_f - 1.0, 1.0)
    )
    shape = (degree_count, lat_total, orders.shape[0])
    general = degree >= order_rows + 2
    step_one = degree == order_rows + 1
    at_start = degree == order_rows
    zero_map = jnp.zeros(shape, jnp.float32)
    first_row = jnp.where(
        general, ratio_a * cosine, jnp.where(step_one, jnp.sqrt(2.0 * morder + 3.0) * cosine, 0.0)
    )
    second_entry = jnp.where(general, -ratio_a * ratio_b, 0.0) + zero_map
    lower_entry = jnp.where(degree > order_rows, 1.0, 0.0) + zero_map
    offset = jnp.where(at_start, diagonal, 0.0)
    elements = (first_row, second_entry, lower_entry, zero_map, offset, zero_map)
    composed = lax.associative_scan(compose_maps, elements, axis=0)
    return jnp.transpose(composed[4], (1, 2, 0))


def latitude_weights(lat_total):
    colatitude = (jnp.arange(lat_total, dtype=jnp.float32) + 0.5) * (math.pi / lat_total)
    return jnp.sin(colatitude) * (math.pi / lat_total)


def forward_table(lon_cells, order_count):
    lon_index = jnp.arange(lon_cells, dtype=jnp.int32)[:, None]
    order_index = jnp.arange(order_count, dtype=jnp.int32)[None, :]
    angles = (lon_index * order_index % lon_cells).astype(jnp.float32) * (2.0 * math.pi / lon_cells)
    factor = 2.0 * math.pi / lon_cells
    return jnp.concatenate([jnp.cos(angles) * factor, -jnp.sin(angles) * factor], axis=1).astype(
        jnp.bfloat16
    )


def inverse_table(lon_cells, order_count):
    order_index = jnp.arange(order_count, dtype=jnp.int32)[:, None]
    lon_index = jnp.arange(lon_cells, dtype=jnp.int32)[None, :]
    angles = (lon_index * order_index % lon_cells).astype(jnp.float32) * (2.0 * math.pi / lon_cells)
    factor = jnp.where(order_index == 0, 1.0, 2.0)
    return jnp.concatenate([factor * jnp.cos(angles), -factor * jnp.sin(angles)], axis=0).astype(
        jnp.bfloat16
    )


def gelu_slope(preact):
    return (
        0.5 * (1.0 + lax.erf(preact * 0.7071067811865476))
        + preact * jnp.exp(-0.5 * preact * preact) * 0.3989422804014327
    )


def shards(field, filters, weight_in, weight_out, norm_gain, cotangent):
    lat_count = lax.axis_size("lat")
    position = lax.axis_index("lat")
    members, lat_rows, lon_cells, channels = field.shape
    degrees = lat_rows * lat_count
    orders = position * lat_rows + jnp.arange(lat_rows, dtype=jnp.int32)
    legendre_table = legendre(degrees, orders, degrees)
    synth_table = legendre_table.astype(jnp.bfloat16)
    analysis_table = (latitude_weights(degrees)[:, None, None] * legendre_table).astype(
        jnp.bfloat16
    )
    forward = forward_table(lon_cells, degrees)
    inverse = inverse_table(lon_cells, degrees)

    def to_orders(values):
        pieces = values.reshape(members, lat_rows, 2, lat_count, lat_rows, channels)
        arrived = lax.all_to_all(pieces, "lat", split_axis=3, concat_axis=1, tiled=True)
        return arrived.reshape(members, degrees, 2, lat_rows, channels)

    def to_grid(values):
        pieces = values.reshape(members, degrees, 2, 1, lat_rows, channels)
        arrived = lax.all_to_all(pieces, "lat", split_axis=1, concat_axis=3, tiled=True)
        return arrived.reshape(members, lat_rows, 2 * degrees, channels)

    def analyze(table, values):
        return jnp.einsum("jkl,bjrkc->brklc", table, values, preferred_element_type=jnp.float32)

    def synthesize(table, coeffs):
        return jnp.einsum("jkl,brklc->bjrkc", table, coeffs, preferred_element_type=jnp.float32)

    spectral = jnp.einsum(
        "bjkc,kn->bjnc", field, forward, preferred_element_type=jnp.float32
    ).astype(jnp.bfloat16)
    spectral_orders = to_orders(spectral)
    coeffs = analyze(analysis_table, spectral_orders).astype(jnp.bfloat16)
    coeffs_f32 = coeffs.astype(jnp.float32)
    spectral_gain = filters.astype(jnp.float32)
    real_part = coeffs_f32[:, 0] * spectral_gain[0] - coeffs_f32[:, 1] * spectral_gain[1]
    imag_part = coeffs_f32[:, 0] * spectral_gain[1] + coeffs_f32[:, 1] * spectral_gain[0]
    filtered = jnp.stack([real_part, imag_part], axis=1).astype(jnp.bfloat16)
    synthesized = synthesize(synth_table, filtered).astype(jnp.bfloat16)
    grid_side = to_grid(synthesized)
    back = jnp.einsum("bjnc,nk->bjkc", grid_side, inverse, preferred_element_type=jnp.float32)
    summed = (field.astype(jnp.float32) + back).astype(jnp.bfloat16)
    summed_f32 = summed.astype(jnp.float32)
    average = jnp.mean(summed_f32, axis=-1, keepdims=True)
    centered = summed_f32 - average
    inverse_std = lax.rsqrt(jnp.mean(centered * centered, axis=-1, keepdims=True) + EPSILON)
    normal = centered * inverse_std
    normed = (normal * norm_gain).astype(jnp.bfloat16)
    preact = jnp.einsum("bjkc,ch->bjkh", normed, weight_in, preferred_element_type=jnp.float32)
    hidden = jax.nn.gelu(preact, approximate=False).astype(jnp.bfloat16)
    block_out = (
        summed_f32
        + jnp.einsum("bjkh,hc->bjkc", hidden, weight_out, preferred_element_type=jnp.float32)
    ).astype(jnp.bfloat16)
    grad_pre = (
        jnp.einsum("bjkc,hc->bjkh", cotangent, weight_out, preferred_element_type=jnp.float32)
        * gelu_slope(preact)
    ).astype(jnp.bfloat16)
    grad_weight_in = jnp.einsum(
        "bjkc,bjkh->ch", normed, grad_pre, preferred_element_type=jnp.float32
    )
    grad_weight_out = jnp.einsum(
        "bjkh,bjkc->hc", hidden, cotangent, preferred_element_type=jnp.float32
    )
    grad_normed = jnp.einsum(
        "bjkh,ch->bjkc", grad_pre, weight_in, preferred_element_type=jnp.float32
    )
    grad_gain = jnp.sum(grad_normed * normal, axis=(0, 1, 2))
    grad_normal = grad_normed * norm_gain
    grad_summed = cotangent.astype(jnp.float32) + inverse_std * (
        grad_normal
        - jnp.mean(grad_normal, axis=-1, keepdims=True)
        - normal * jnp.mean(grad_normal * normal, axis=-1, keepdims=True)
    )
    grad_rounded = grad_summed.astype(jnp.bfloat16)
    grad_synth = jnp.einsum(
        "bjkc,nk->bjnc", grad_rounded, inverse, preferred_element_type=jnp.float32
    ).astype(jnp.bfloat16)
    grad_orders = to_orders(grad_synth)
    grad_filtered = analyze(synth_table, grad_orders)
    grad_real = grad_filtered[:, 0]
    grad_imag = grad_filtered[:, 1]
    filter_real = jnp.sum(coeffs_f32[:, 0] * grad_real + coeffs_f32[:, 1] * grad_imag, axis=(0, 1))
    filter_imag = jnp.sum(coeffs_f32[:, 0] * grad_imag - coeffs_f32[:, 1] * grad_real, axis=(0, 1))
    grad_filters = jnp.stack([filter_real, filter_imag], axis=0)
    coeff_real = grad_real * spectral_gain[0] + grad_imag * spectral_gain[1]
    coeff_imag = grad_imag * spectral_gain[0] - grad_real * spectral_gain[1]
    grad_coeffs = jnp.stack([coeff_real, coeff_imag], axis=1).astype(jnp.bfloat16)
    grad_spectral = synthesize(analysis_table, grad_coeffs).astype(jnp.bfloat16)
    grad_grid = to_grid(grad_spectral)
    grad_field = (
        grad_summed
        + jnp.einsum("bjnc,kn->bjkc", grad_grid, forward, preferred_element_type=jnp.float32)
    ).astype(jnp.bfloat16)
    grad_filters, grad_weight_in, grad_weight_out, grad_gain = lax.psum(
        (grad_filters, grad_weight_in, grad_weight_out, grad_gain), "lat"
    )
    grad_scale = 1.0 / math.sqrt(members * degrees * lon_cells)
    return (
        block_out,
        grad_field,
        grad_filters * grad_scale,
        grad_weight_in * grad_scale,
        grad_weight_out * grad_scale,
        grad_gain * grad_scale,
    )


HALF = 128
SLOT = 8
TILE = 16
MESH = pl.DeviceIdType.MESH


def dot(a, b):
    return jnp.dot(a, b, preferred_element_type=jnp.float32)


def dot_nt(a, b):
    return lax.dot_general(a, b, (((1,), (1,)), ((), ())), preferred_element_type=jnp.float32)


def dot_tn(a, b):
    return lax.dot_general(a, b, (((0,), (0,)), ((), ())), preferred_element_type=jnp.float32)


def fused_kernel(
    n, rows, lon, scale,
    field, filters, w_in, w_out, gain, cot, fwd_nk, inv_kn, inv_nk, fwd_kn, tables,
    block_out, grad_field, grad_filters, grad_w_in, grad_w_out, grad_gain,
    send, recv, fsend, frecv, fgather, wsend, wpair, wchips, wrecv, wgather,
    table, up, summed, normed, hidden, grad_pre, grad_sum, coeffs,
    x0, x1, y0, y1, f0, f1, nat,
    send_sem, recv_sem, chip_send, chip_recv, pair_send, pair_recv, table_sem,
):
    me = lax.axis_index("lat")
    ens = lax.axis_index("ens")
    core = lax.rem(me, 2)
    chip = me // 2
    chips = n // 2
    partner = me + 1 - 2 * core
    degrees = n * rows
    bf16 = jnp.bfloat16

    barrier = pltpu.get_barrier_semaphore()

    def greet(k, _):
        pl.semaphore_signal(
            barrier, inc=1, device_id=(ens, lax.rem(me + k, n)), device_id_type=MESH
        )
        return 0

    lax.fori_loop(1, n, greet, 0)
    fetch = pltpu.make_async_copy(tables.at[me], table, table_sem)
    fetch.start()

    def exchange(phase, source, target):
        def copy(k):
            to = lax.rem(me + k, n)
            return pltpu.make_async_remote_copy(
                src_ref=source(to), dst_ref=target(me),
                send_sem=send_sem.at[phase, k], recv_sem=recv_sem.at[phase, k],
                device_id=(ens, to), device_id_type=MESH,
            )

        def landing(k):
            origin = lax.rem(me + n - k, n)
            return pltpu.make_async_remote_copy(
                src_ref=source(origin), dst_ref=target(origin),
                send_sem=send_sem.at[phase, k], recv_sem=recv_sem.at[phase, k],
                device_id=(ens, origin), device_id_type=MESH,
            )

        def start(k, _):
            copy(k).start()
            return 0

        def arrive(k, _):
            landing(k).wait_recv()
            return 0

        def leave(k, _):
            copy(k).wait_send()
            return 0

        return (
            lambda: lax.fori_loop(1, n, start, 0),
            lambda: lax.fori_loop(1, n, arrive, 0),
            lambda: lax.fori_loop(1, n, leave, 0),
        )

    def all_to_all(phase):
        return exchange(phase, lambda i: send.at[phase, i], lambda i: recv.at[phase, i])

    def pack_grid(phase, parts):
        pieces = [p[:, h : h + HALF].reshape(n, SLOT, HALF) for h in (0, HALF) for p in parts]
        send[phase] = jnp.concatenate(pieces, axis=1).astype(bf16)
        recv[phase, me] = send[phase, me]

    def pack_orders(phase):
        y = [v[...].reshape(n, rows * SLOT, HALF) for v in (y0, y1)]
        send[phase] = jnp.concatenate(y, axis=1).astype(bf16)
        recv[phase, me] = send[phase, me]

    def unpack_orders(phase):
        arrived = recv[phase].astype(jnp.float32)
        x0[...] = arrived[:, : rows * SLOT].reshape(degrees * SLOT, HALF)
        x1[...] = arrived[:, rows * SLOT :].reshape(degrees * SLOT, HALF)

    def unpack_grid(phase, j):
        parts = [
            recv[phase, :, pl.ds(0, 2 * rows * SLOT), :].astype(jnp.float32)[
                :, (h * rows + j) * SLOT : (h * rows + j + 1) * SLOT
            ].reshape(n * SLOT, HALF)
            for h in (0, 1)
        ]
        return jnp.concatenate(parts, axis=1).astype(bf16)

    def of_order(m):
        picked = [
            v[pl.ds(r * rows + m, degrees, stride=SLOT), :] for r in (0, 1) for v in (x0, x1)
        ]
        return jnp.concatenate(picked, axis=1).astype(bf16)

    def to_order(m, value):
        for r in (0, 1):
            for h, v in enumerate((y0, y1)):
                at = (2 * r + h) * HALF
                v[pl.ds(r * rows + m, degrees, stride=SLOT), :] = value[:, at : at + HALF]

    start0, arrive0, leave0 = all_to_all(0)
    pack_grid(0, [dot(fwd_nk[...], field[pl.ds(j * lon, lon), :]) for j in range(rows)])
    pl.semaphore_wait(barrier, n - 1)
    start0()
    y0[...] = jnp.zeros_like(y0)
    y1[...] = jnp.zeros_like(y1)
    f0[...] = jnp.zeros_like(f0)
    f1[...] = jnp.zeros_like(f1)
    for j in range(rows):
        at = pl.ds(j * lon, lon)
        up[at, :] = dot_nt(cot[at, :], w_out[...])
    fetch.wait()
    g0 = filters[0].astype(jnp.float32)
    g1 = filters[1].astype(jnp.float32)
    wide = 2 * HALF
    arrive0()

    start1, arrive1, leave1 = all_to_all(1)
    unpack_orders(0)
    for m in range(rows):
        c = dot(table[0, m], of_order(m)).astype(bf16)
        coeffs[m] = c
        c = c.astype(jnp.float32)
        cr, ci = c[:, :wide], c[:, wide:]
        filtered = jnp.concatenate([cr * g0 - ci * g1, cr * g1 + ci * g0], axis=1).astype(bf16)
        to_order(m, dot(table[1, m], filtered))
    pack_orders(1)
    start1()
    arrive1()

    start2, arrive2, leave2 = all_to_all(2)
    gain_row = gain[...]
    gain_sum = jnp.zeros_like(gain_row)
    parts = []
    for j in range(rows):
        at = pl.ds(j * lon, lon)
        back = dot(inv_kn[...], unpack_grid(1, j))
        s = (field[at, :].astype(jnp.float32) + back).astype(bf16)
        summed[at, :] = s
        s = s.astype(jnp.float32)
        centered = s - jnp.mean(s, axis=-1, keepdims=True)
        inverse_std = lax.rsqrt(jnp.mean(centered * centered, axis=-1, keepdims=True) + EPSILON)
        normal = centered * inverse_std
        nb = (normal * gain_row).astype(bf16)
        normed[at, :] = nb
        pre = dot(nb, w_in[...])
        phi = 0.5 * (1.0 + lax.erf(pre * 0.7071067811865476))
        hidden[at, :] = (pre * phi).astype(bf16)
        slope = phi + pre * jnp.exp(-0.5 * pre * pre) * 0.3989422804014327
        gp = (up[at, :] * slope).astype(bf16)
        grad_pre[at, :] = gp
        gn = dot_nt(gp, w_in[...])
        gain_sum = gain_sum + jnp.sum(gn * normal, axis=0, keepdims=True)
        v = gn * gain_row
        gs = cot[at, :].astype(jnp.float32) + inverse_std * (
            v
            - jnp.mean(v, axis=-1, keepdims=True)
            - normal * jnp.mean(v * normal, axis=-1, keepdims=True)
        )
        grad_sum[at, :] = gs
        parts.append(dot(inv_nk[...], gs.astype(bf16)))
    pack_grid(2, parts)
    start2()

    mid = w_in.shape[0] // n
    gi = dot_tn(normed[...], grad_pre[...]).astype(bf16)
    wsend[:, :, :mid, :] = gi.reshape(2, chips, mid, gi.shape[1])
    go = dot_tn(hidden[...], cot[...]).astype(bf16).reshape(2, chips, 2 * mid, w_out.shape[1])
    wsend[:, :, mid:, :] = jnp.concatenate([go[:, :, :mid], go[:, :, mid:]], axis=3)

    def pair_copy(slot, source, target):
        return pltpu.make_async_remote_copy(
            src_ref=source, dst_ref=target,
            send_sem=pair_send.at[slot], recv_sem=pair_recv.at[slot],
            device_id=(ens, partner), device_id_type=MESH,
        )

    def chip_exchange(phase, source, target):
        def copy(k):
            to = lax.rem(chip + k, chips)
            return pltpu.make_async_remote_copy(
                src_ref=source(to), dst_ref=target(chip),
                send_sem=chip_send.at[phase, k], recv_sem=chip_recv.at[phase, k],
                device_id=(ens, 2 * to + core), device_id_type=MESH,
            )

        def landing(k):
            origin = lax.rem(chip + chips - k, chips)
            return pltpu.make_async_remote_copy(
                src_ref=source(origin), dst_ref=target(origin),
                send_sem=chip_send.at[phase, k], recv_sem=chip_recv.at[phase, k],
                device_id=(ens, 2 * origin + core), device_id_type=MESH,
            )

        def start(k, _):
            copy(k).start()
            return 0

        def arrive(k, _):
            landing(k).wait_recv()
            return 0

        def leave(k, _):
            copy(k).wait_send()
            return 0

        return (
            lambda: lax.fori_loop(1, chips, start, 0),
            lambda: lax.fori_loop(1, chips, arrive, 0),
            lambda: lax.fori_loop(1, chips, leave, 0),
        )

    pair0 = pair_copy(0, wsend.at[1 - core], wpair)
    pair0.start()
    for j in range(rows):
        at = pl.ds(j * lon, lon)
        block_out[at, :] = (
            summed[at, :].astype(jnp.float32) + dot(hidden[at, :], w_out[...])
        ).astype(bf16)
    pair0.wait_recv()
    scatter_start, scatter_arrive, scatter_leave = chip_exchange(
        0, lambda i: wchips.at[i], lambda i: wrecv.at[i]
    )
    wchips[...] = (wsend[core].astype(jnp.float32) + wpair[...].astype(jnp.float32)).astype(bf16)
    wrecv[chip] = wchips[chip]
    scatter_start()

    arrive2()
    start3, arrive3, leave3 = all_to_all(3)
    unpack_orders(2)
    fr = jnp.zeros((degrees, wide), jnp.float32)
    fi = jnp.zeros((degrees, wide), jnp.float32)
    for m in range(rows):
        g = dot(table[2, m], of_order(m))
        gr, gi = g[:, :wide], g[:, wide:]
        c = coeffs[m].astype(jnp.float32)
        cr, ci = c[:, :wide], c[:, wide:]
        fr = fr + (cr * gr + ci * gi)
        fi = fi + (cr * gi - ci * gr)
        gc = jnp.concatenate([gr * g0 + gi * g1, gi * g0 - gr * g1], axis=1).astype(bf16)
        to_order(m, dot(table[3, m], gc))
    pack_orders(3)
    start3()

    for r, f in enumerate((fr, fi)):
        for h in (0, 1):
            nat[2 * r + h] = f[:, h * HALF : (h + 1) * HALF]
    for h, f in enumerate((f0, f1)):
        for r in (0, 1):
            for m in range(rows):
                f[pl.ds(r * rows + m, n, stride=SLOT), :] = nat[
                    2 * r + h, pl.ds(m, n, stride=rows), :
                ]
        f[pl.ds(2 * rows, n, stride=SLOT), :] = jnp.broadcast_to(
            gain_sum[:, h * HALF : (h + 1) * HALF], (n, HALF)
        )
    fsend[...] = jnp.concatenate(
        [f[...].reshape(n, SLOT, HALF) for f in (f0, f1)], axis=1
    ).astype(bf16)
    frecv[me] = fsend[me]
    start4, arrive4, leave4 = exchange(4, lambda i: fsend.at[i], lambda i: frecv.at[i])
    start4()

    gather_start, gather_arrive, gather_leave = chip_exchange(
        1, lambda i: wgather.at[core, chip], lambda i: wgather.at[core, i]
    )
    scatter_arrive()
    wgather[core, chip] = jnp.sum(wrecv[...].astype(jnp.float32), axis=0).astype(bf16)
    gather_start()

    arrive4()
    ftotal = jnp.sum(frecv[...].astype(jnp.float32), axis=0)
    grad_gain[...] = scale * jnp.concatenate(
        [ftotal[2 * rows : 2 * rows + 1], ftotal[SLOT + 2 * rows : SLOT + 2 * rows + 1]], axis=1
    )
    fgather[me] = ftotal.astype(bf16)
    start5, arrive5, leave5 = exchange(5, lambda i: fgather.at[me], lambda i: fgather.at[i])
    start5()

    arrive3()
    for j in range(rows):
        at = pl.ds(j * lon, lon)
        grad_field[at, :] = (grad_sum[at, :] + dot(fwd_kn[...], unpack_grid(3, j))).astype(bf16)

    gather_arrive()
    pair1 = pair_copy(1, wgather.at[core], wgather.at[core])
    pair1_in = pair_copy(1, wgather.at[1 - core], wgather.at[1 - core])
    pair1.start()

    arrive5()
    fall = fgather[...].astype(jnp.float32) * scale
    f0[...] = fall[:, :SLOT].reshape(n * SLOT, HALF)
    f1[...] = fall[:, SLOT:].reshape(n * SLOT, HALF)
    for h, f in enumerate((f0, f1)):
        for r in (0, 1):
            for m in range(rows):
                nat[2 * r + h, pl.ds(m, n, stride=rows), :] = f[
                    pl.ds(r * rows + m, n, stride=SLOT), :
                ]
            grad_filters[r, :, h * HALF : (h + 1) * HALF] = nat[2 * r + h]

    pair1_in.wait_recv()
    full = w_in.shape[1]
    for c in (0, 1):
        grad_w_in[pl.ds(c * chips * mid, chips * mid), :] = (
            wgather[c, :, :mid, :].astype(jnp.float32) * scale
        ).reshape(chips * mid, full)
        both = wgather[c, :, mid:, :].astype(jnp.float32) * scale
        grad_w_out[pl.ds(2 * c * chips * mid, 2 * chips * mid), :] = jnp.concatenate(
            [both[:, :, : full // 2], both[:, :, full // 2 :]], axis=1
        ).reshape(2 * chips * mid, full // 2)

    for leave in (leave0, leave1, leave2, leave3, leave4, leave5, scatter_leave, gather_leave):
        leave()
    pair0.wait_send()
    pair1.wait_send()


def legendre_constants(total):
    theta = (np.arange(total) + 0.5) * (math.pi / total)
    x, sine = np.cos(theta), np.sin(theta)
    p = np.zeros((total, total, total), np.float64)
    for m in range(total):
        log_start = 0.5 * (
            math.log((2.0 * m + 1.0) / (4.0 * math.pi))
            + math.lgamma(m + 0.5)
            - math.lgamma(m + 1.0)
            - 0.5 * math.log(math.pi)
        )
        p[:, m, m] = np.exp(log_start + m * np.log(sine))
        if m + 1 < total:
            p[:, m, m + 1] = math.sqrt(2.0 * m + 3.0) * x * p[:, m, m]
        for l in range(m + 2, total):
            a = math.sqrt((4.0 * l * l - 1.0) / (l * l - m * m))
            b = math.sqrt(((l - 1.0) ** 2 - m * m) / (4.0 * (l - 1.0) ** 2 - 1.0))
            p[:, m, l] = a * (x * p[:, m, l - 1] - b * p[:, m, l - 2])
    weights = sine * (math.pi / total)
    return p, weights[:, None, None] * p


def slot_rows(table, n, rows):
    lon = table.shape[2]
    spread = np.zeros((n, SLOT, lon), np.float64)
    spread[:, : 2 * rows] = (
        table.reshape(2, n, rows, lon).transpose(1, 0, 2, 3).reshape(n, 2 * rows, lon)
    )
    return spread.reshape(n * SLOT, lon)


def fused_constants(n, rows, lon):
    total = n * rows
    synth, analysis = legendre_constants(total)
    by_owner = lambda t, axes: t.transpose(axes).reshape(n, rows, total, total)
    tables = np.stack(
        [
            by_owner(analysis, (1, 2, 0)),
            by_owner(synth, (1, 0, 2)),
            by_owner(synth, (1, 2, 0)),
            by_owner(analysis, (1, 0, 2)),
        ],
        axis=1,
    )
    angle = (np.arange(total)[:, None] * np.arange(lon)[None, :] % lon) * (2.0 * math.pi / lon)
    wave = np.stack([np.cos(angle), -np.sin(angle)])
    forward = slot_rows(wave * (2.0 * math.pi / lon), n, rows)
    inverse = slot_rows(wave * np.where(np.arange(total) == 0, 1.0, 2.0)[:, None], n, rows)
    cast = lambda t: np.asarray(t, np.float32).astype(ml_dtypes.bfloat16)
    return (
        cast(forward), cast(inverse.T), cast(inverse), cast(forward.T), cast(tables),
    )


def fused(field, filters, weight_in, weight_out, norm_gain, cotangent):
    n = lax.axis_size("lat")
    _, rows, lon, channels = field.shape
    hid = weight_in.shape[1]
    cells, total, chips = rows * lon, rows * n, n // 2
    mid = channels // n
    f32, bf16 = jnp.float32, jnp.bfloat16
    scale = 1.0 / math.sqrt(total * lon)
    constants = fused_constants(n, rows, lon)
    vmem = pl.BlockSpec(memory_space=pltpu.VMEM)
    phases = 4
    outs = pl.pallas_call(
        functools.partial(fused_kernel, n, rows, lon, scale),
        out_shape=(
            jax.ShapeDtypeStruct((cells, channels), bf16),
            jax.ShapeDtypeStruct((cells, channels), bf16),
            jax.ShapeDtypeStruct((2, total, channels), f32),
            jax.ShapeDtypeStruct((channels, hid), f32),
            jax.ShapeDtypeStruct((hid, channels), f32),
            jax.ShapeDtypeStruct((1, channels), f32),
        ),
        in_specs=[vmem] * 10 + [pl.BlockSpec(memory_space=pl.ANY)],
        out_specs=(vmem,) * 6,
        scratch_shapes=[
            pltpu.VMEM((phases, n, 2 * rows * SLOT, HALF), bf16),
            pltpu.VMEM((phases, n, 2 * rows * SLOT, HALF), bf16),
            pltpu.VMEM((n, 2 * SLOT, HALF), bf16),
            pltpu.VMEM((n, 2 * SLOT, HALF), bf16),
            pltpu.VMEM((n, 2 * SLOT, HALF), bf16),
            pltpu.VMEM((2, chips, 2 * mid, hid), bf16),
            pltpu.VMEM((chips, 2 * mid, hid), bf16),
            pltpu.VMEM((chips, 2 * mid, hid), bf16),
            pltpu.VMEM((chips, 2 * mid, hid), bf16),
            pltpu.VMEM((2, chips, 2 * mid, hid), bf16),
            pltpu.VMEM((4, rows, total, total), bf16),
            pltpu.VMEM((cells, hid), f32),
            pltpu.VMEM((cells, channels), bf16),
            pltpu.VMEM((cells, channels), bf16),
            pltpu.VMEM((cells, hid), bf16),
            pltpu.VMEM((cells, hid), bf16),
            pltpu.VMEM((cells, channels), f32),
            pltpu.VMEM((rows, total, 2 * channels), bf16),
            pltpu.VMEM((total * SLOT, HALF), f32),
            pltpu.VMEM((total * SLOT, HALF), f32),
            pltpu.VMEM((total * SLOT, HALF), f32),
            pltpu.VMEM((total * SLOT, HALF), f32),
            pltpu.VMEM((n * SLOT, HALF), f32),
            pltpu.VMEM((n * SLOT, HALF), f32),
            pltpu.VMEM((4, total, HALF), f32),
            pltpu.SemaphoreType.DMA((6, n)),
            pltpu.SemaphoreType.DMA((6, n)),
            pltpu.SemaphoreType.DMA((2, chips)),
            pltpu.SemaphoreType.DMA((2, chips)),
            pltpu.SemaphoreType.DMA((2,)),
            pltpu.SemaphoreType.DMA((2,)),
            pltpu.SemaphoreType.DMA,
        ],
        compiler_params=pltpu.CompilerParams(
            collective_id=0, has_side_effects=True, vmem_limit_bytes=40 * 1024 * 1024
        ),
    )(
        field.reshape(cells, channels), filters, weight_in, weight_out,
        norm_gain.reshape(1, channels), cotangent.reshape(cells, channels),
        *[jnp.asarray(t) for t in constants],
    )
    return (
        outs[0].reshape(field.shape), outs[1].reshape(field.shape),
        outs[2], outs[3], outs[4], outs[5].reshape(channels),
    )


def block(field, filters, weight_in, weight_out, norm_gain, cotangent):
    n = lax.axis_size("lat")
    members, rows, lon, channels = field.shape
    hid = weight_in.shape[1]
    fits = (
        members == 1
        and n % 2 == 0
        and 2 * rows < SLOT
        and channels == 2 * HALF
        and hid == 2 * channels
        and channels % (TILE * n) == 0
        and (rows * n) % TILE == 0
        and lon % TILE == 0
        and rows * lon * hid <= 512 * 1024
    )
    chosen = fused if fits else shards
    return chosen(field, filters, weight_in, weight_out, norm_gain, cotangent)


def solution(mesh):
    placed = (P("ens", "lat", None, None), P(), P(), P(), P(), P("ens", "lat", None, None))
    return jax.shard_map(
        block,
        mesh=mesh,
        in_specs=placed,
        out_specs=(
            P("ens", "lat", None, None),
            P("ens", "lat", None, None),
            P("ens", None, None),
            P("ens", None),
            P("ens", None),
            P("ens"),
        ),
        check_vma=False,
    )
```

```python
import functools
import math

import jax
import jax.numpy as jnp
import ml_dtypes
import numpy as np
from jax import lax
from jax.experimental import pallas as pl
from jax.experimental.pallas import tpu as pltpu
from jax.sharding import PartitionSpec as P

EPSILON = 1e-05


def compose_maps(earlier, later):
    e00, e01, e10, e11, ec0, ec1 = earlier
    l00, l01, l10, l11, lc0, lc1 = later
    return (
        l00 * e00 + l01 * e10,
        l00 * e01 + l01 * e11,
        l10 * e00 + l11 * e10,
        l10 * e01 + l11 * e11,
        l00 * ec0 + l01 * ec1 + lc0,
        l10 * ec0 + l11 * ec1 + lc1,
    )


def legendre(lat_total, orders, degree_count):
    colatitude = (jnp.arange(lat_total, dtype=jnp.float32) + 0.5) * (math.pi / lat_total)
    cosine = jnp.cos(colatitude)[None, :, None]
    sine_theta = jnp.sin(colatitude)[:, None]
    morder_row = orders.astype(jnp.float32)[None, :]
    log_start = 0.5 * (
        jnp.log((2.0 * morder_row + 1.0) / (4.0 * math.pi))
        + lax.lgamma(morder_row + 0.5)
        - lax.lgamma(morder_row + 1.0)
        - 0.5 * math.log(math.pi)
    ) + morder_row * jnp.log(sine_theta)
    diagonal = jnp.exp(log_start)[None, :, :]
    morder = orders.astype(jnp.float32)[None, None, :]
    order_rows = orders[None, None, :]
    degree = jnp.arange(degree_count, dtype=jnp.int32)[:, None, None]
    degree_f = degree.astype(jnp.float32)
    ratio_a = jnp.sqrt(
        (4.0 * degree_f * degree_f - 1.0) / jnp.maximum(degree_f * degree_f - morder * morder, 1.0)
    )
    previous_f = degree_f - 1.0
    ratio_b = jnp.sqrt(
        jnp.maximum(previous_f * previous_f - morder * morder, 0.0)
        / jnp.maximum(4.0 * previous_f * previous_f - 1.0, 1.0)
    )
    shape = (degree_count, lat_total, orders.shape[0])
    general = degree >= order_rows + 2
    step_one = degree == order_rows + 1
    at_start = degree == order_rows
    zero_map = jnp.zeros(shape, jnp.float32)
    first_row = jnp.where(
        general, ratio_a * cosine, jnp.where(step_one, jnp.sqrt(2.0 * morder + 3.0) * cosine, 0.0)
    )
    second_entry = jnp.where(general, -ratio_a * ratio_b, 0.0) + zero_map
    lower_entry = jnp.where(degree > order_rows, 1.0, 0.0) + zero_map
    offset = jnp.where(at_start, diagonal, 0.0)
    elements = (first_row, second_entry, lower_entry, zero_map, offset, zero_map)
    composed = lax.associative_scan(compose_maps, elements, axis=0)
    return jnp.transpose(composed[4], (1, 2, 0))


def latitude_weights(lat_total):
    colatitude = (jnp.arange(lat_total, dtype=jnp.float32) + 0.5) * (math.pi / lat_total)
    return jnp.sin(colatitude) * (math.pi / lat_total)


def forward_table(lon_cells, order_count):
    lon_index = jnp.arange(lon_cells, dtype=jnp.int32)[:, None]
    order_index = jnp.arange(order_count, dtype=jnp.int32)[None, :]
    angles = (lon_index * order_index % lon_cells).astype(jnp.float32) * (2.0 * math.pi / lon_cells)
    factor = 2.0 * math.pi / lon_cells
    return jnp.concatenate([jnp.cos(angles) * factor, -jnp.sin(angles) * factor], axis=1).astype(
        jnp.bfloat16
    )


def inverse_table(lon_cells, order_count):
    order_index = jnp.arange(order_count, dtype=jnp.int32)[:, None]
    lon_index = jnp.arange(lon_cells, dtype=jnp.int32)[None, :]
    angles = (lon_index * order_index % lon_cells).astype(jnp.float32) * (2.0 * math.pi / lon_cells)
    factor = jnp.where(order_index == 0, 1.0, 2.0)
    return jnp.concatenate([factor * jnp.cos(angles), -factor * jnp.sin(angles)], axis=0).astype(
        jnp.bfloat16
    )


def gelu_slope(preact):
    return (
        0.5 * (1.0 + lax.erf(preact * 0.7071067811865476))
        + preact * jnp.exp(-0.5 * preact * preact) * 0.3989422804014327
    )


def shards(field, filters, weight_in, weight_out, norm_gain, cotangent):
    lat_count = lax.axis_size("lat")
    position = lax.axis_index("lat")
    members, lat_rows, lon_cells, channels = field.shape
    degrees = lat_rows * lat_count
    orders = position * lat_rows + jnp.arange(lat_rows, dtype=jnp.int32)
    legendre_table = legendre(degrees, orders, degrees)
    synth_table = legendre_table.astype(jnp.bfloat16)
    analysis_table = (latitude_weights(degrees)[:, None, None] * legendre_table).astype(
        jnp.bfloat16
    )
    forward = forward_table(lon_cells, degrees)
    inverse = inverse_table(lon_cells, degrees)

    def to_orders(values):
        pieces = values.reshape(members, lat_rows, 2, lat_count, lat_rows, channels)
        arrived = lax.all_to_all(pieces, "lat", split_axis=3, concat_axis=1, tiled=True)
        return arrived.reshape(members, degrees, 2, lat_rows, channels)

    def to_grid(values):
        pieces = values.reshape(members, degrees, 2, 1, lat_rows, channels)
        arrived = lax.all_to_all(pieces, "lat", split_axis=1, concat_axis=3, tiled=True)
        return arrived.reshape(members, lat_rows, 2 * degrees, channels)

    def analyze(table, values):
        return jnp.einsum("jkl,bjrkc->brklc", table, values, preferred_element_type=jnp.float32)

    def synthesize(table, coeffs):
        return jnp.einsum("jkl,brklc->bjrkc", table, coeffs, preferred_element_type=jnp.float32)

    spectral = jnp.einsum(
        "bjkc,kn->bjnc", field, forward, preferred_element_type=jnp.float32
    ).astype(jnp.bfloat16)
    spectral_orders = to_orders(spectral)
    coeffs = analyze(analysis_table, spectral_orders).astype(jnp.bfloat16)
    coeffs_f32 = coeffs.astype(jnp.float32)
    spectral_gain = filters.astype(jnp.float32)
    real_part = coeffs_f32[:, 0] * spectral_gain[0] - coeffs_f32[:, 1] * spectral_gain[1]
    imag_part = coeffs_f32[:, 0] * spectral_gain[1] + coeffs_f32[:, 1] * spectral_gain[0]
    filtered = jnp.stack([real_part, imag_part], axis=1).astype(jnp.bfloat16)
    synthesized = synthesize(synth_table, filtered).astype(jnp.bfloat16)
    grid_side = to_grid(synthesized)
    back = jnp.einsum("bjnc,nk->bjkc", grid_side, inverse, preferred_element_type=jnp.float32)
    summed = (field.astype(jnp.float32) + back).astype(jnp.bfloat16)
    summed_f32 = summed.astype(jnp.float32)
    average = jnp.mean(summed_f32, axis=-1, keepdims=True)
    centered = summed_f32 - average
    inverse_std = lax.rsqrt(jnp.mean(centered * centered, axis=-1, keepdims=True) + EPSILON)
    normal = centered * inverse_std
    normed = (normal * norm_gain).astype(jnp.bfloat16)
    preact = jnp.einsum("bjkc,ch->bjkh", normed, weight_in, preferred_element_type=jnp.float32)
    hidden = jax.nn.gelu(preact, approximate=False).astype(jnp.bfloat16)
    block_out = (
        summed_f32
        + jnp.einsum("bjkh,hc->bjkc", hidden, weight_out, preferred_element_type=jnp.float32)
    ).astype(jnp.bfloat16)
    grad_pre = (
        jnp.einsum("bjkc,hc->bjkh", cotangent, weight_out, preferred_element_type=jnp.float32)
        * gelu_slope(preact)
    ).astype(jnp.bfloat16)
    grad_weight_in = jnp.einsum(
        "bjkc,bjkh->ch", normed, grad_pre, preferred_element_type=jnp.float32
    )
    grad_weight_out = jnp.einsum(
        "bjkh,bjkc->hc", hidden, cotangent, preferred_element_type=jnp.float32
    )
    grad_normed = jnp.einsum(
        "bjkh,ch->bjkc", grad_pre, weight_in, preferred_element_type=jnp.float32
    )
    grad_gain = jnp.sum(grad_normed * normal, axis=(0, 1, 2))
    grad_normal = grad_normed * norm_gain
    grad_summed = cotangent.astype(jnp.float32) + inverse_std * (
        grad_normal
        - jnp.mean(grad_normal, axis=-1, keepdims=True)
        - normal * jnp.mean(grad_normal * normal, axis=-1, keepdims=True)
    )
    grad_rounded = grad_summed.astype(jnp.bfloat16)
    grad_synth = jnp.einsum(
        "bjkc,nk->bjnc", grad_rounded, inverse, preferred_element_type=jnp.float32
    ).astype(jnp.bfloat16)
    grad_orders = to_orders(grad_synth)
    grad_filtered = analyze(synth_table, grad_orders)
    grad_real = grad_filtered[:, 0]
    grad_imag = grad_filtered[:, 1]
    filter_real = jnp.sum(coeffs_f32[:, 0] * grad_real + coeffs_f32[:, 1] * grad_imag, axis=(0, 1))
    filter_imag = jnp.sum(coeffs_f32[:, 0] * grad_imag - coeffs_f32[:, 1] * grad_real, axis=(0, 1))
    grad_filters = jnp.stack([filter_real, filter_imag], axis=0)
    coeff_real = grad_real * spectral_gain[0] + grad_imag * spectral_gain[1]
    coeff_imag = grad_imag * spectral_gain[0] - grad_real * spectral_gain[1]
    grad_coeffs = jnp.stack([coeff_real, coeff_imag], axis=1).astype(jnp.bfloat16)
    grad_spectral = synthesize(analysis_table, grad_coeffs).astype(jnp.bfloat16)
    grad_grid = to_grid(grad_spectral)
    grad_field = (
        grad_summed
        + jnp.einsum("bjnc,kn->bjkc", grad_grid, forward, preferred_element_type=jnp.float32)
    ).astype(jnp.bfloat16)
    grad_filters, grad_weight_in, grad_weight_out, grad_gain = lax.psum(
        (grad_filters, grad_weight_in, grad_weight_out, grad_gain), "lat"
    )
    grad_scale = 1.0 / math.sqrt(members * degrees * lon_cells)
    return (
        block_out,
        grad_field,
        grad_filters * grad_scale,
        grad_weight_in * grad_scale,
        grad_weight_out * grad_scale,
        grad_gain * grad_scale,
    )


HALF = 128
SLOT = 8
TILE = 16
VMEM_LIMIT = 62 * 1024 * 1024
MESH = pl.DeviceIdType.MESH


def dot(a, b):
    return jnp.dot(a, b, preferred_element_type=jnp.float32)


def dot_nt(a, b):
    return lax.dot_general(a, b, (((1,), (1,)), ((), ())), preferred_element_type=jnp.float32)


def dot_tn(a, b):
    return lax.dot_general(a, b, (((0,), (0,)), ((), ())), preferred_element_type=jnp.float32)


def fused_kernel(
    n, rows, lon, scale,
    field_in, filters_in, w_in_in, w_out_in, gain_in, cot_in, fwd_nk_in, inv_kn_in, inv_nk_in,
    fwd_kn_in, tables,
    block_out_to, grad_field_to, grad_filters_to, grad_gain_to, weights_to,
    send, recv, fsend, frecv, fgather, wsend, wpair, wchips, wrecv, wgather,
    table, up, summed, normed, hidden, grad_pre, grad_sum, coeffs,
    x0, x1, y0, y1, f0, f1, nat,
    field, filters, w_in, w_out, gain, cot, fwd_nk, inv_kn, inv_nk, fwd_kn,
    block_out, grad_field, grad_filters, grad_gain,
    send_sem, recv_sem, chip_send, chip_recv, pair_send, pair_recv, fetch_sem, store_sem,
):
    me = lax.axis_index("lat")
    ens = lax.axis_index("ens")
    core = lax.rem(me, 2)
    chip = me // 2
    chips = n // 2
    partner = me + 1 - 2 * core
    degrees = n * rows
    bf16 = jnp.bfloat16

    barrier = pltpu.get_barrier_semaphore()

    def greet(k, _):
        pl.semaphore_signal(
            barrier, inc=1, device_id=(ens, lax.rem(me + k, n)), device_id_type=MESH
        )
        return 0

    fetches = [
        pltpu.make_async_copy(source, target, fetch_sem.at[i])
        for i, (source, target) in enumerate(
            (
                (field_in, field), (fwd_nk_in, fwd_nk), (cot_in, cot), (w_out_in, w_out),
                (tables.at[me], table), (filters_in, filters), (inv_kn_in, inv_kn),
                (w_in_in, w_in), (gain_in, gain), (inv_nk_in, inv_nk), (fwd_kn_in, fwd_kn),
            )
        )
    ]
    for fetch in fetches:
        fetch.start()
    lax.fori_loop(1, n, greet, 0)

    stores = [
        pltpu.make_async_copy(source, target, store_sem.at[i])
        for i, (source, target) in enumerate(
            (
                (block_out, block_out_to), (grad_field, grad_field_to),
                (grad_filters, grad_filters_to), (grad_gain, grad_gain_to),
                (wgather, weights_to),
            )
        )
    ]

    def exchange(phase, source, target):
        def copy(k):
            to = lax.rem(me + k, n)
            return pltpu.make_async_remote_copy(
                src_ref=source(to), dst_ref=target(me),
                send_sem=send_sem.at[phase, k], recv_sem=recv_sem.at[phase, k],
                device_id=(ens, to), device_id_type=MESH,
            )

        def landing(k):
            origin = lax.rem(me + n - k, n)
            return pltpu.make_async_remote_copy(
                src_ref=source(origin), dst_ref=target(origin),
                send_sem=send_sem.at[phase, k], recv_sem=recv_sem.at[phase, k],
                device_id=(ens, origin), device_id_type=MESH,
            )

        def start(k, _):
            copy(k).start()
            return 0

        def arrive(k, _):
            landing(k).wait_recv()
            return 0

        def leave(k, _):
            copy(k).wait_send()
            return 0

        return (
            lambda: lax.fori_loop(1, n, start, 0),
            lambda: lax.fori_loop(1, n, arrive, 0),
            lambda: lax.fori_loop(1, n, leave, 0),
        )

    def all_to_all(phase):
        return exchange(phase, lambda i: send.at[phase, i], lambda i: recv.at[phase, i])

    def pack_grid(phase, parts):
        pieces = [p[:, h : h + HALF].reshape(n, SLOT, HALF) for h in (0, HALF) for p in parts]
        send[phase] = jnp.concatenate(pieces, axis=1).astype(bf16)
        recv[phase, me] = send[phase, me]

    def pack_orders(phase):
        y = [v[...].reshape(n, rows * SLOT, HALF) for v in (y0, y1)]
        send[phase] = jnp.concatenate(y, axis=1).astype(bf16)
        recv[phase, me] = send[phase, me]

    def unpack_orders(phase):
        arrived = recv[phase].astype(jnp.float32)
        x0[...] = arrived[:, : rows * SLOT].reshape(degrees * SLOT, HALF)
        x1[...] = arrived[:, rows * SLOT :].reshape(degrees * SLOT, HALF)

    def unpack_grid(phase, j):
        parts = [
            recv[phase, :, pl.ds(0, 2 * rows * SLOT), :].astype(jnp.float32)[
                :, (h * rows + j) * SLOT : (h * rows + j + 1) * SLOT
            ].reshape(n * SLOT, HALF)
            for h in (0, 1)
        ]
        return jnp.concatenate(parts, axis=1).astype(bf16)

    def of_order(m):
        picked = [
            v[pl.ds(r * rows + m, degrees, stride=SLOT), :] for r in (0, 1) for v in (x0, x1)
        ]
        return jnp.concatenate(picked, axis=1).astype(bf16)

    def to_order(m, value):
        for r in (0, 1):
            for h, v in enumerate((y0, y1)):
                at = (2 * r + h) * HALF
                v[pl.ds(r * rows + m, degrees, stride=SLOT), :] = value[:, at : at + HALF]

    start0, arrive0, leave0 = all_to_all(0)
    for fetch in fetches[:2]:
        fetch.wait()
    pack_grid(0, [dot(fwd_nk[...], field[pl.ds(j * lon, lon), :]) for j in range(rows)])
    pl.semaphore_wait(barrier, n - 1)
    start0()
    y0[...] = jnp.zeros_like(y0)
    y1[...] = jnp.zeros_like(y1)
    f0[...] = jnp.zeros_like(f0)
    f1[...] = jnp.zeros_like(f1)
    for fetch in fetches[2:]:
        fetch.wait()
    for j in range(rows):
        at = pl.ds(j * lon, lon)
        up[at, :] = dot_nt(cot[at, :], w_out[...])
    g0 = filters[0].astype(jnp.float32)
    g1 = filters[1].astype(jnp.float32)
    wide = 2 * HALF
    arrive0()

    start1, arrive1, leave1 = all_to_all(1)
    unpack_orders(0)
    for m in range(rows):
        c = dot(table[0, m], of_order(m)).astype(bf16)
        coeffs[m] = c
        c = c.astype(jnp.float32)
        cr, ci = c[:, :wide], c[:, wide:]
        filtered = jnp.concatenate([cr * g0 - ci * g1, cr * g1 + ci * g0], axis=1).astype(bf16)
        to_order(m, dot(table[1, m], filtered))
    pack_orders(1)
    start1()
    arrive1()

    start2, arrive2, leave2 = all_to_all(2)
    gain_row = gain[...]
    gain_sum = jnp.zeros_like(gain_row)
    parts = []
    for j in range(rows):
        at = pl.ds(j * lon, lon)
        back = dot(inv_kn[...], unpack_grid(1, j))
        s = (field[at, :].astype(jnp.float32) + back).astype(bf16)
        summed[at, :] = s
        s = s.astype(jnp.float32)
        centered = s - jnp.mean(s, axis=-1, keepdims=True)
        inverse_std = lax.rsqrt(jnp.mean(centered * centered, axis=-1, keepdims=True) + EPSILON)
        normal = centered * inverse_std
        nb = (normal * gain_row).astype(bf16)
        normed[at, :] = nb
        pre = dot(nb, w_in[...])
        phi = 0.5 * (1.0 + lax.erf(pre * 0.7071067811865476))
        hidden[at, :] = (pre * phi).astype(bf16)
        slope = phi + pre * jnp.exp(-0.5 * pre * pre) * 0.3989422804014327
        gp = (up[at, :] * slope).astype(bf16)
        grad_pre[at, :] = gp
        gn = dot_nt(gp, w_in[...])
        gain_sum = gain_sum + jnp.sum(gn * normal, axis=0, keepdims=True)
        v = gn * gain_row
        gs = cot[at, :].astype(jnp.float32) + inverse_std * (
            v
            - jnp.mean(v, axis=-1, keepdims=True)
            - normal * jnp.mean(v * normal, axis=-1, keepdims=True)
        )
        grad_sum[at, :] = gs
        parts.append(dot(inv_nk[...], gs.astype(bf16)))
    pack_grid(2, parts)
    start2()

    mid = w_in.shape[0] // n
    gi = dot_tn(normed[...], grad_pre[...]).astype(bf16)
    wsend[:, :, :mid, :] = gi.reshape(2, chips, mid, gi.shape[1])
    go = dot_tn(hidden[...], cot[...]).astype(bf16).reshape(2, chips, 2 * mid, w_out.shape[1])
    wsend[:, :, mid:, :] = jnp.concatenate([go[:, :, :mid], go[:, :, mid:]], axis=3)

    def pair_copy(slot, source, target):
        return pltpu.make_async_remote_copy(
            src_ref=source, dst_ref=target,
            send_sem=pair_send.at[slot], recv_sem=pair_recv.at[slot],
            device_id=(ens, partner), device_id_type=MESH,
        )

    def chip_exchange(phase, source, target):
        def copy(k):
            to = lax.rem(chip + k, chips)
            return pltpu.make_async_remote_copy(
                src_ref=source(to), dst_ref=target(chip),
                send_sem=chip_send.at[phase, k], recv_sem=chip_recv.at[phase, k],
                device_id=(ens, 2 * to + core), device_id_type=MESH,
            )

        def landing(k):
            origin = lax.rem(chip + chips - k, chips)
            return pltpu.make_async_remote_copy(
                src_ref=source(origin), dst_ref=target(origin),
                send_sem=chip_send.at[phase, k], recv_sem=chip_recv.at[phase, k],
                device_id=(ens, 2 * origin + core), device_id_type=MESH,
            )

        def start(k, _):
            copy(k).start()
            return 0

        def arrive(k, _):
            landing(k).wait_recv()
            return 0

        def leave(k, _):
            copy(k).wait_send()
            return 0

        return (
            lambda: lax.fori_loop(1, chips, start, 0),
            lambda: lax.fori_loop(1, chips, arrive, 0),
            lambda: lax.fori_loop(1, chips, leave, 0),
        )

    pair0 = pair_copy(0, wsend.at[1 - core], wpair)
    pair0.start()
    for j in range(rows):
        at = pl.ds(j * lon, lon)
        block_out[at, :] = (
            summed[at, :].astype(jnp.float32) + dot(hidden[at, :], w_out[...])
        ).astype(bf16)
    stores[0].start()
    pair0.wait_recv()
    scatter_start, scatter_arrive, scatter_leave = chip_exchange(
        0, lambda i: wchips.at[i], lambda i: wrecv.at[i]
    )
    wchips[...] = (wsend[core].astype(jnp.float32) + wpair[...].astype(jnp.float32)).astype(bf16)
    wrecv[chip] = wchips[chip]
    scatter_start()

    arrive2()
    start3, arrive3, leave3 = all_to_all(3)
    unpack_orders(2)
    fr = jnp.zeros((degrees, wide), jnp.float32)
    fi = jnp.zeros((degrees, wide), jnp.float32)
    for m in range(rows):
        g = dot(table[2, m], of_order(m))
        gr, gi = g[:, :wide], g[:, wide:]
        c = coeffs[m].astype(jnp.float32)
        cr, ci = c[:, :wide], c[:, wide:]
        fr = fr + (cr * gr + ci * gi)
        fi = fi + (cr * gi - ci * gr)
        gc = jnp.concatenate([gr * g0 + gi * g1, gi * g0 - gr * g1], axis=1).astype(bf16)
        to_order(m, dot(table[3, m], gc))
    pack_orders(3)
    start3()

    for r, f in enumerate((fr, fi)):
        for h in (0, 1):
            nat[2 * r + h] = f[:, h * HALF : (h + 1) * HALF]
    for h, f in enumerate((f0, f1)):
        for r in (0, 1):
            for m in range(rows):
                f[pl.ds(r * rows + m, n, stride=SLOT), :] = nat[
                    2 * r + h, pl.ds(m, n, stride=rows), :
                ]
        f[pl.ds(2 * rows, n, stride=SLOT), :] = jnp.broadcast_to(
            gain_sum[:, h * HALF : (h + 1) * HALF], (n, HALF)
        )
    fsend[...] = jnp.concatenate(
        [f[...].reshape(n, SLOT, HALF) for f in (f0, f1)], axis=1
    ).astype(bf16)
    frecv[me] = fsend[me]
    start4, arrive4, leave4 = exchange(4, lambda i: fsend.at[i], lambda i: frecv.at[i])
    start4()

    gather_start, gather_arrive, gather_leave = chip_exchange(
        1, lambda i: wgather.at[core, chip], lambda i: wgather.at[core, i]
    )
    scatter_arrive()
    wgather[core, chip] = jnp.sum(wrecv[...].astype(jnp.float32), axis=0).astype(bf16)
    gather_start()

    arrive4()
    ftotal = jnp.sum(frecv[...].astype(jnp.float32), axis=0)
    grad_gain[...] = scale * jnp.concatenate(
        [ftotal[2 * rows : 2 * rows + 1], ftotal[SLOT + 2 * rows : SLOT + 2 * rows + 1]], axis=1
    )
    stores[3].start()
    fgather[me] = ftotal.astype(bf16)
    start5, arrive5, leave5 = exchange(5, lambda i: fgather.at[me], lambda i: fgather.at[i])
    start5()

    arrive3()
    for j in range(rows):
        at = pl.ds(j * lon, lon)
        grad_field[at, :] = (grad_sum[at, :] + dot(fwd_kn[...], unpack_grid(3, j))).astype(bf16)

    stores[1].start()

    gather_arrive()
    pair1 = pair_copy(1, wgather.at[core], wgather.at[core])
    pair1_in = pair_copy(1, wgather.at[1 - core], wgather.at[1 - core])
    pair1.start()

    arrive5()
    fall = fgather[...].astype(jnp.float32) * scale
    f0[...] = fall[:, :SLOT].reshape(n * SLOT, HALF)
    f1[...] = fall[:, SLOT:].reshape(n * SLOT, HALF)
    for h, f in enumerate((f0, f1)):
        for r in (0, 1):
            for m in range(rows):
                nat[2 * r + h, pl.ds(m, n, stride=rows), :] = f[
                    pl.ds(r * rows + m, n, stride=SLOT), :
                ]
            grad_filters[r, :, h * HALF : (h + 1) * HALF] = nat[2 * r + h]

    stores[2].start()
    pair1_in.wait_recv()
    stores[4].start()
    for leave in (leave0, leave1, leave2, leave3, leave4, leave5, scatter_leave, gather_leave):
        leave()
    pair0.wait_send()
    pair1.wait_send()
    for store in stores:
        store.wait()


def write_kernel(scale, *refs):
    count = 5
    sources, refs = refs[:count], refs[count:]
    targets, refs = refs[: count + 1], refs[count + 1 :]
    held, (grad_w_in, grad_w_out, in_sem, out_sem) = refs[:count], refs[count:]
    wgather = held[-1]
    loads = [
        pltpu.make_async_copy(sources[i], held[i], in_sem.at[i]) for i in range(count)
    ]
    stores = [
        pltpu.make_async_copy(source, targets[i], out_sem.at[i])
        for i, source in enumerate((*held[:-1], grad_w_in, grad_w_out))
    ]
    for load in reversed(loads):
        load.start()
    loads[-1].wait()
    _, chips, double, full = wgather.shape
    mid = double // 2
    for c in (0, 1):
        grad_w_in[pl.ds(c * chips * mid, chips * mid), :] = (
            wgather[c, :, :mid, :].astype(jnp.float32) * scale
        ).reshape(chips * mid, full)
        both = wgather[c, :, mid:, :].astype(jnp.float32) * scale
        grad_w_out[pl.ds(2 * c * chips * mid, 2 * chips * mid), :] = jnp.concatenate(
            [both[:, :, : full // 2], both[:, :, full // 2 :]], axis=1
        ).reshape(2 * chips * mid, full // 2)
    stores[-1].start()
    stores[-2].start()
    for i in range(count - 1):
        loads[i].wait()
        stores[i].start()
    for store in stores:
        store.wait()


def legendre_constants(total):
    theta = (np.arange(total) + 0.5) * (math.pi / total)
    x, sine = np.cos(theta), np.sin(theta)
    p = np.zeros((total, total, total), np.float64)
    for m in range(total):
        log_start = 0.5 * (
            math.log((2.0 * m + 1.0) / (4.0 * math.pi))
            + math.lgamma(m + 0.5)
            - math.lgamma(m + 1.0)
            - 0.5 * math.log(math.pi)
        )
        p[:, m, m] = np.exp(log_start + m * np.log(sine))
        if m + 1 < total:
            p[:, m, m + 1] = math.sqrt(2.0 * m + 3.0) * x * p[:, m, m]
        for l in range(m + 2, total):
            a = math.sqrt((4.0 * l * l - 1.0) / (l * l - m * m))
            b = math.sqrt(((l - 1.0) ** 2 - m * m) / (4.0 * (l - 1.0) ** 2 - 1.0))
            p[:, m, l] = a * (x * p[:, m, l - 1] - b * p[:, m, l - 2])
    weights = sine * (math.pi / total)
    return p, weights[:, None, None] * p


def slot_rows(table, n, rows):
    lon = table.shape[2]
    spread = np.zeros((n, SLOT, lon), np.float64)
    spread[:, : 2 * rows] = (
        table.reshape(2, n, rows, lon).transpose(1, 0, 2, 3).reshape(n, 2 * rows, lon)
    )
    return spread.reshape(n * SLOT, lon)


def fused_constants(n, rows, lon):
    total = n * rows
    synth, analysis = legendre_constants(total)
    by_owner = lambda t, axes: t.transpose(axes).reshape(n, rows, total, total)
    tables = np.stack(
        [
            by_owner(analysis, (1, 2, 0)),
            by_owner(synth, (1, 0, 2)),
            by_owner(synth, (1, 2, 0)),
            by_owner(analysis, (1, 0, 2)),
        ],
        axis=1,
    )
    angle = (np.arange(total)[:, None] * np.arange(lon)[None, :] % lon) * (2.0 * math.pi / lon)
    wave = np.stack([np.cos(angle), -np.sin(angle)])
    forward = slot_rows(wave * (2.0 * math.pi / lon), n, rows)
    inverse = slot_rows(wave * np.where(np.arange(total) == 0, 1.0, 2.0)[:, None], n, rows)
    cast = lambda t: np.asarray(t, np.float32).astype(ml_dtypes.bfloat16)
    return (
        cast(forward), cast(inverse.T), cast(inverse), cast(forward.T), cast(tables),
    )


def fused(field, filters, weight_in, weight_out, norm_gain, cotangent):
    n = lax.axis_size("lat")
    _, rows, lon, channels = field.shape
    hid = weight_in.shape[1]
    cells, total, chips = rows * lon, rows * n, n // 2
    mid = channels // n
    f32, bf16 = jnp.float32, jnp.bfloat16
    scale = 1.0 / math.sqrt(total * lon)
    constants = fused_constants(n, rows, lon)
    hbm = pl.BlockSpec(memory_space=pltpu.HBM)
    phases = 4
    outs = pl.pallas_call(
        functools.partial(fused_kernel, n, rows, lon, scale),
        out_shape=(
            jax.ShapeDtypeStruct((cells, channels), bf16),
            jax.ShapeDtypeStruct((cells, channels), bf16),
            jax.ShapeDtypeStruct((2, total, channels), f32),
            jax.ShapeDtypeStruct((1, channels), f32),
            jax.ShapeDtypeStruct((2, chips, 2 * mid, hid), bf16),
        ),
        in_specs=[hbm] * 11,
        out_specs=(hbm,) * 5,
        scratch_shapes=[
            pltpu.VMEM((phases, n, 2 * rows * SLOT, HALF), bf16),
            pltpu.VMEM((phases, n, 2 * rows * SLOT, HALF), bf16),
            pltpu.VMEM((n, 2 * SLOT, HALF), bf16),
            pltpu.VMEM((n, 2 * SLOT, HALF), bf16),
            pltpu.VMEM((n, 2 * SLOT, HALF), bf16),
            pltpu.VMEM((2, chips, 2 * mid, hid), bf16),
            pltpu.VMEM((chips, 2 * mid, hid), bf16),
            pltpu.VMEM((chips, 2 * mid, hid), bf16),
            pltpu.VMEM((chips, 2 * mid, hid), bf16),
            pltpu.VMEM((2, chips, 2 * mid, hid), bf16),
            pltpu.VMEM((4, rows, total, total), bf16),
            pltpu.VMEM((cells, hid), f32),
            pltpu.VMEM((cells, channels), bf16),
            pltpu.VMEM((cells, channels), bf16),
            pltpu.VMEM((cells, hid), bf16),
            pltpu.VMEM((cells, hid), bf16),
            pltpu.VMEM((cells, channels), f32),
            pltpu.VMEM((rows, total, 2 * channels), bf16),
            pltpu.VMEM((total * SLOT, HALF), f32),
            pltpu.VMEM((total * SLOT, HALF), f32),
            pltpu.VMEM((total * SLOT, HALF), f32),
            pltpu.VMEM((total * SLOT, HALF), f32),
            pltpu.VMEM((n * SLOT, HALF), f32),
            pltpu.VMEM((n * SLOT, HALF), f32),
            pltpu.VMEM((4, total, HALF), f32),
            pltpu.VMEM((cells, channels), bf16),
            pltpu.VMEM(filters.shape, bf16),
            pltpu.VMEM(weight_in.shape, bf16),
            pltpu.VMEM(weight_out.shape, bf16),
            pltpu.VMEM((1, channels), f32),
            pltpu.VMEM((cells, channels), bf16),
            *[pltpu.VMEM(t.shape, bf16) for t in constants[:4]],
            pltpu.VMEM((cells, channels), bf16),
            pltpu.VMEM((cells, channels), bf16),
            pltpu.VMEM((2, total, channels), f32),
            pltpu.VMEM((1, channels), f32),
            pltpu.SemaphoreType.DMA((6, n)),
            pltpu.SemaphoreType.DMA((6, n)),
            pltpu.SemaphoreType.DMA((2, chips)),
            pltpu.SemaphoreType.DMA((2, chips)),
            pltpu.SemaphoreType.DMA((2,)),
            pltpu.SemaphoreType.DMA((2,)),
            pltpu.SemaphoreType.DMA((11,)),
            pltpu.SemaphoreType.DMA((5,)),
        ],
        compiler_params=pltpu.CompilerParams(
            collective_id=0, has_side_effects=True, vmem_limit_bytes=VMEM_LIMIT
        ),
    )(
        field.reshape(cells, channels), filters, weight_in, weight_out,
        norm_gain.reshape(1, channels), cotangent.reshape(cells, channels),
        *[jnp.asarray(t) for t in constants],
    )
    weight_shapes = ((channels, hid), (hid, channels))
    outs = pl.pallas_call(
        functools.partial(write_kernel, scale),
        out_shape=(
            *[jax.ShapeDtypeStruct(o.shape, o.dtype) for o in outs[:-1]],
            *[jax.ShapeDtypeStruct(shape, f32) for shape in weight_shapes],
        ),
        in_specs=[hbm] * 5,
        out_specs=(hbm,) * 6,
        scratch_shapes=[
            *[pltpu.VMEM(o.shape, o.dtype) for o in outs],
            *[pltpu.VMEM(shape, f32) for shape in weight_shapes],
            pltpu.SemaphoreType.DMA((5,)),
            pltpu.SemaphoreType.DMA((6,)),
        ],
        compiler_params=pltpu.CompilerParams(vmem_limit_bytes=VMEM_LIMIT),
    )(*outs)
    return (
        outs[0].reshape(field.shape), outs[1].reshape(field.shape),
        outs[2], outs[4], outs[5], outs[3].reshape(channels),
    )


def block(field, filters, weight_in, weight_out, norm_gain, cotangent):
    n = lax.axis_size("lat")
    members, rows, lon, channels = field.shape
    hid = weight_in.shape[1]
    fits = (
        members == 1
        and n % 2 == 0
        and 2 * rows < SLOT
        and channels == 2 * HALF
        and hid == 2 * channels
        and channels % (TILE * n) == 0
        and (rows * n) % TILE == 0
        and lon % TILE == 0
        and rows * lon * hid <= 512 * 1024
    )
    chosen = fused if fits else shards
    return chosen(field, filters, weight_in, weight_out, norm_gain, cotangent)


def solution(mesh):
    placed = (P("ens", "lat", None, None), P(), P(), P(), P(), P("ens", "lat", None, None))
    return jax.shard_map(
        block,
        mesh=mesh,
        in_specs=placed,
        out_specs=(
            P("ens", "lat", None, None),
            P("ens", "lat", None, None),
            P("ens", None, None),
            P("ens", None),
            P("ens", None),
            P("ens"),
        ),
        check_vma=False,
    )
```

```python
import functools
import math

import jax
import jax.numpy as jnp
import ml_dtypes
import numpy as np
from jax import lax
from jax.experimental import pallas as pl
from jax.experimental.pallas import tpu as pltpu
from jax.sharding import PartitionSpec as P

EPSILON = 1e-05


def compose_maps(earlier, later):
    e00, e01, e10, e11, ec0, ec1 = earlier
    l00, l01, l10, l11, lc0, lc1 = later
    return (
        l00 * e00 + l01 * e10,
        l00 * e01 + l01 * e11,
        l10 * e00 + l11 * e10,
        l10 * e01 + l11 * e11,
        l00 * ec0 + l01 * ec1 + lc0,
        l10 * ec0 + l11 * ec1 + lc1,
    )


def legendre(lat_total, orders, degree_count):
    colatitude = (jnp.arange(lat_total, dtype=jnp.float32) + 0.5) * (math.pi / lat_total)
    cosine = jnp.cos(colatitude)[None, :, None]
    sine_theta = jnp.sin(colatitude)[:, None]
    morder_row = orders.astype(jnp.float32)[None, :]
    log_start = 0.5 * (
        jnp.log((2.0 * morder_row + 1.0) / (4.0 * math.pi))
        + lax.lgamma(morder_row + 0.5)
        - lax.lgamma(morder_row + 1.0)
        - 0.5 * math.log(math.pi)
    ) + morder_row * jnp.log(sine_theta)
    diagonal = jnp.exp(log_start)[None, :, :]
    morder = orders.astype(jnp.float32)[None, None, :]
    order_rows = orders[None, None, :]
    degree = jnp.arange(degree_count, dtype=jnp.int32)[:, None, None]
    degree_f = degree.astype(jnp.float32)
    ratio_a = jnp.sqrt(
        (4.0 * degree_f * degree_f - 1.0) / jnp.maximum(degree_f * degree_f - morder * morder, 1.0)
    )
    previous_f = degree_f - 1.0
    ratio_b = jnp.sqrt(
        jnp.maximum(previous_f * previous_f - morder * morder, 0.0)
        / jnp.maximum(4.0 * previous_f * previous_f - 1.0, 1.0)
    )
    shape = (degree_count, lat_total, orders.shape[0])
    general = degree >= order_rows + 2
    step_one = degree == order_rows + 1
    at_start = degree == order_rows
    zero_map = jnp.zeros(shape, jnp.float32)
    first_row = jnp.where(
        general, ratio_a * cosine, jnp.where(step_one, jnp.sqrt(2.0 * morder + 3.0) * cosine, 0.0)
    )
    second_entry = jnp.where(general, -ratio_a * ratio_b, 0.0) + zero_map
    lower_entry = jnp.where(degree > order_rows, 1.0, 0.0) + zero_map
    offset = jnp.where(at_start, diagonal, 0.0)
    elements = (first_row, second_entry, lower_entry, zero_map, offset, zero_map)
    composed = lax.associative_scan(compose_maps, elements, axis=0)
    return jnp.transpose(composed[4], (1, 2, 0))


def latitude_weights(lat_total):
    colatitude = (jnp.arange(lat_total, dtype=jnp.float32) + 0.5) * (math.pi / lat_total)
    return jnp.sin(colatitude) * (math.pi / lat_total)


def forward_table(lon_cells, order_count):
    lon_index = jnp.arange(lon_cells, dtype=jnp.int32)[:, None]
    order_index = jnp.arange(order_count, dtype=jnp.int32)[None, :]
    angles = (lon_index * order_index % lon_cells).astype(jnp.float32) * (2.0 * math.pi / lon_cells)
    factor = 2.0 * math.pi / lon_cells
    return jnp.concatenate([jnp.cos(angles) * factor, -jnp.sin(angles) * factor], axis=1).astype(
        jnp.bfloat16
    )


def inverse_table(lon_cells, order_count):
    order_index = jnp.arange(order_count, dtype=jnp.int32)[:, None]
    lon_index = jnp.arange(lon_cells, dtype=jnp.int32)[None, :]
    angles = (lon_index * order_index % lon_cells).astype(jnp.float32) * (2.0 * math.pi / lon_cells)
    factor = jnp.where(order_index == 0, 1.0, 2.0)
    return jnp.concatenate([factor * jnp.cos(angles), -factor * jnp.sin(angles)], axis=0).astype(
        jnp.bfloat16
    )


def gelu_slope(preact):
    return (
        0.5 * (1.0 + lax.erf(preact * 0.7071067811865476))
        + preact * jnp.exp(-0.5 * preact * preact) * 0.3989422804014327
    )


def shards(field, filters, weight_in, weight_out, norm_gain, cotangent):
    lat_count = lax.axis_size("lat")
    position = lax.axis_index("lat")
    members, lat_rows, lon_cells, channels = field.shape
    degrees = lat_rows * lat_count
    orders = position * lat_rows + jnp.arange(lat_rows, dtype=jnp.int32)
    legendre_table = legendre(degrees, orders, degrees)
    synth_table = legendre_table.astype(jnp.bfloat16)
    analysis_table = (latitude_weights(degrees)[:, None, None] * legendre_table).astype(
        jnp.bfloat16
    )
    forward = forward_table(lon_cells, degrees)
    inverse = inverse_table(lon_cells, degrees)

    def to_orders(values):
        pieces = values.reshape(members, lat_rows, 2, lat_count, lat_rows, channels)
        arrived = lax.all_to_all(pieces, "lat", split_axis=3, concat_axis=1, tiled=True)
        return arrived.reshape(members, degrees, 2, lat_rows, channels)

    def to_grid(values):
        pieces = values.reshape(members, degrees, 2, 1, lat_rows, channels)
        arrived = lax.all_to_all(pieces, "lat", split_axis=1, concat_axis=3, tiled=True)
        return arrived.reshape(members, lat_rows, 2 * degrees, channels)

    def analyze(table, values):
        return jnp.einsum("jkl,bjrkc->brklc", table, values, preferred_element_type=jnp.float32)

    def synthesize(table, coeffs):
        return jnp.einsum("jkl,brklc->bjrkc", table, coeffs, preferred_element_type=jnp.float32)

    spectral = jnp.einsum(
        "bjkc,kn->bjnc", field, forward, preferred_element_type=jnp.float32
    ).astype(jnp.bfloat16)
    spectral_orders = to_orders(spectral)
    coeffs = analyze(analysis_table, spectral_orders).astype(jnp.bfloat16)
    coeffs_f32 = coeffs.astype(jnp.float32)
    spectral_gain = filters.astype(jnp.float32)
    real_part = coeffs_f32[:, 0] * spectral_gain[0] - coeffs_f32[:, 1] * spectral_gain[1]
    imag_part = coeffs_f32[:, 0] * spectral_gain[1] + coeffs_f32[:, 1] * spectral_gain[0]
    filtered = jnp.stack([real_part, imag_part], axis=1).astype(jnp.bfloat16)
    synthesized = synthesize(synth_table, filtered).astype(jnp.bfloat16)
    grid_side = to_grid(synthesized)
    back = jnp.einsum("bjnc,nk->bjkc", grid_side, inverse, preferred_element_type=jnp.float32)
    summed = (field.astype(jnp.float32) + back).astype(jnp.bfloat16)
    summed_f32 = summed.astype(jnp.float32)
    average = jnp.mean(summed_f32, axis=-1, keepdims=True)
    centered = summed_f32 - average
    inverse_std = lax.rsqrt(jnp.mean(centered * centered, axis=-1, keepdims=True) + EPSILON)
    normal = centered * inverse_std
    normed = (normal * norm_gain).astype(jnp.bfloat16)
    preact = jnp.einsum("bjkc,ch->bjkh", normed, weight_in, preferred_element_type=jnp.float32)
    hidden = jax.nn.gelu(preact, approximate=False).astype(jnp.bfloat16)
    block_out = (
        summed_f32
        + jnp.einsum("bjkh,hc->bjkc", hidden, weight_out, preferred_element_type=jnp.float32)
    ).astype(jnp.bfloat16)
    grad_pre = (
        jnp.einsum("bjkc,hc->bjkh", cotangent, weight_out, preferred_element_type=jnp.float32)
        * gelu_slope(preact)
    ).astype(jnp.bfloat16)
    grad_weight_in = jnp.einsum(
        "bjkc,bjkh->ch", normed, grad_pre, preferred_element_type=jnp.float32
    )
    grad_weight_out = jnp.einsum(
        "bjkh,bjkc->hc", hidden, cotangent, preferred_element_type=jnp.float32
    )
    grad_normed = jnp.einsum(
        "bjkh,ch->bjkc", grad_pre, weight_in, preferred_element_type=jnp.float32
    )
    grad_gain = jnp.sum(grad_normed * normal, axis=(0, 1, 2))
    grad_normal = grad_normed * norm_gain
    grad_summed = cotangent.astype(jnp.float32) + inverse_std * (
        grad_normal
        - jnp.mean(grad_normal, axis=-1, keepdims=True)
        - normal * jnp.mean(grad_normal * normal, axis=-1, keepdims=True)
    )
    grad_rounded = grad_summed.astype(jnp.bfloat16)
    grad_synth = jnp.einsum(
        "bjkc,nk->bjnc", grad_rounded, inverse, preferred_element_type=jnp.float32
    ).astype(jnp.bfloat16)
    grad_orders = to_orders(grad_synth)
    grad_filtered = analyze(synth_table, grad_orders)
    grad_real = grad_filtered[:, 0]
    grad_imag = grad_filtered[:, 1]
    filter_real = jnp.sum(coeffs_f32[:, 0] * grad_real + coeffs_f32[:, 1] * grad_imag, axis=(0, 1))
    filter_imag = jnp.sum(coeffs_f32[:, 0] * grad_imag - coeffs_f32[:, 1] * grad_real, axis=(0, 1))
    grad_filters = jnp.stack([filter_real, filter_imag], axis=0)
    coeff_real = grad_real * spectral_gain[0] + grad_imag * spectral_gain[1]
    coeff_imag = grad_imag * spectral_gain[0] - grad_real * spectral_gain[1]
    grad_coeffs = jnp.stack([coeff_real, coeff_imag], axis=1).astype(jnp.bfloat16)
    grad_spectral = synthesize(analysis_table, grad_coeffs).astype(jnp.bfloat16)
    grad_grid = to_grid(grad_spectral)
    grad_field = (
        grad_summed
        + jnp.einsum("bjnc,kn->bjkc", grad_grid, forward, preferred_element_type=jnp.float32)
    ).astype(jnp.bfloat16)
    grad_filters, grad_weight_in, grad_weight_out, grad_gain = lax.psum(
        (grad_filters, grad_weight_in, grad_weight_out, grad_gain), "lat"
    )
    grad_scale = 1.0 / math.sqrt(members * degrees * lon_cells)
    return (
        block_out,
        grad_field,
        grad_filters * grad_scale,
        grad_weight_in * grad_scale,
        grad_weight_out * grad_scale,
        grad_gain * grad_scale,
    )


HALF = 128
SLOT = 8
TILE = 16
VMEM_LIMIT = 62 * 1024 * 1024
MESH = pl.DeviceIdType.MESH


def dot(a, b):
    return jnp.dot(a, b, preferred_element_type=jnp.float32)


def dot_nt(a, b):
    return lax.dot_general(a, b, (((1,), (1,)), ((), ())), preferred_element_type=jnp.float32)


def dot_tn(a, b):
    return lax.dot_general(a, b, (((0,), (0,)), ((), ())), preferred_element_type=jnp.float32)


def fused_kernel(
    n, rows, lon, scale,
    field_in, filters_in, w_in_in, w_out_in, gain_in, cot_in, fwd_nk_in, inv_kn_in, inv_nk_in,
    fwd_kn_in, tables,
    block_out_to, grad_field_to, grad_filters_to, grad_gain_to, weights_to,
    send, recv, fsend, frecv, fgather, wsend, wpair, wchips, wrecv, wgather,
    table, up, summed, normed, hidden, grad_pre, grad_sum, coeffs,
    x0, x1, y0, y1, f0, f1, nat,
    field, filters, w_in, w_out, gain, cot, fwd_nk, inv_kn, inv_nk, fwd_kn,
    block_out, grad_field, grad_filters, grad_gain,
    send_sem, recv_sem, chip_send, chip_recv, pair_send, pair_recv, fetch_sem, store_sem,
):
    me = lax.axis_index("lat")
    ens = lax.axis_index("ens")
    core = lax.rem(me, 2)
    chip = me // 2
    chips = n // 2
    partner = me + 1 - 2 * core
    degrees = n * rows
    bf16 = jnp.bfloat16

    barrier = pltpu.get_barrier_semaphore()

    def greet(k, _):
        pl.semaphore_signal(
            barrier, inc=1, device_id=(ens, lax.rem(me + k, n)), device_id_type=MESH
        )
        return 0

    fetches = [
        pltpu.make_async_copy(source, target, fetch_sem.at[i])
        for i, (source, target) in enumerate(
            (
                (field_in, field), (fwd_nk_in, fwd_nk), (cot_in, cot), (w_out_in, w_out),
                (tables.at[me], table), (filters_in, filters), (inv_kn_in, inv_kn),
                (w_in_in, w_in), (gain_in, gain), (inv_nk_in, inv_nk), (fwd_kn_in, fwd_kn),
            )
        )
    ]
    for fetch in fetches:
        fetch.start()
    lax.fori_loop(1, n, greet, 0)

    stores = [
        pltpu.make_async_copy(source, target, store_sem.at[i])
        for i, (source, target) in enumerate(
            (
                (block_out, block_out_to), (grad_field, grad_field_to),
                (grad_filters, grad_filters_to), (grad_gain, grad_gain_to),
                (wgather, weights_to),
            )
        )
    ]

    def exchange(phase, source, target):
        def copy(k):
            to = lax.rem(me + k, n)
            return pltpu.make_async_remote_copy(
                src_ref=source(to), dst_ref=target(me),
                send_sem=send_sem.at[phase, k], recv_sem=recv_sem.at[phase, k],
                device_id=(ens, to), device_id_type=MESH,
            )

        def landing(k):
            origin = lax.rem(me + n - k, n)
            return pltpu.make_async_remote_copy(
                src_ref=source(origin), dst_ref=target(origin),
                send_sem=send_sem.at[phase, k], recv_sem=recv_sem.at[phase, k],
                device_id=(ens, origin), device_id_type=MESH,
            )

        def start(k, _):
            copy(n - k).start()
            return 0

        def arrive(k, _):
            landing(k).wait_recv()
            return 0

        def leave(k, _):
            copy(k).wait_send()
            return 0

        return (
            lambda: lax.fori_loop(1, n, start, 0),
            lambda: lax.fori_loop(1, n, arrive, 0),
            lambda: lax.fori_loop(1, n, leave, 0),
        )

    def all_to_all(phase):
        return exchange(phase, lambda i: send.at[phase, i], lambda i: recv.at[phase, i])

    def pack_grid(phase, parts):
        pieces = [p[:, h : h + HALF].reshape(n, SLOT, HALF) for h in (0, HALF) for p in parts]
        send[phase] = jnp.concatenate(pieces, axis=1).astype(bf16)
        recv[phase, me] = send[phase, me]

    def pack_orders(phase):
        y = [v[...].reshape(n, rows * SLOT, HALF) for v in (y0, y1)]
        send[phase] = jnp.concatenate(y, axis=1).astype(bf16)
        recv[phase, me] = send[phase, me]

    def unpack_orders(phase):
        arrived = recv[phase].astype(jnp.float32)
        x0[...] = arrived[:, : rows * SLOT].reshape(degrees * SLOT, HALF)
        x1[...] = arrived[:, rows * SLOT :].reshape(degrees * SLOT, HALF)

    def unpack_grid(phase, j):
        parts = [
            recv[phase, :, pl.ds(0, 2 * rows * SLOT), :].astype(jnp.float32)[
                :, (h * rows + j) * SLOT : (h * rows + j + 1) * SLOT
            ].reshape(n * SLOT, HALF)
            for h in (0, 1)
        ]
        return jnp.concatenate(parts, axis=1).astype(bf16)

    def of_order(m):
        picked = [
            v[pl.ds(r * rows + m, degrees, stride=SLOT), :] for r in (0, 1) for v in (x0, x1)
        ]
        return jnp.concatenate(picked, axis=1).astype(bf16)

    def to_order(m, value):
        for r in (0, 1):
            for h, v in enumerate((y0, y1)):
                at = (2 * r + h) * HALF
                v[pl.ds(r * rows + m, degrees, stride=SLOT), :] = value[:, at : at + HALF]

    start0, arrive0, leave0 = all_to_all(0)
    for fetch in fetches[:2]:
        fetch.wait()
    pack_grid(0, [dot(fwd_nk[...], field[pl.ds(j * lon, lon), :]) for j in range(rows)])
    pl.semaphore_wait(barrier, n - 1)
    start0()
    y0[...] = jnp.zeros_like(y0)
    y1[...] = jnp.zeros_like(y1)
    f0[...] = jnp.zeros_like(f0)
    f1[...] = jnp.zeros_like(f1)
    for fetch in fetches[2:]:
        fetch.wait()
    for j in range(rows):
        at = pl.ds(j * lon, lon)
        up[at, :] = dot_nt(cot[at, :], w_out[...])
    g0 = filters[0].astype(jnp.float32)
    g1 = filters[1].astype(jnp.float32)
    wide = 2 * HALF
    arrive0()

    start1, arrive1, leave1 = all_to_all(1)
    unpack_orders(0)
    for m in range(rows):
        c = dot(table[0, m], of_order(m)).astype(bf16)
        coeffs[m] = c
        c = c.astype(jnp.float32)
        cr, ci = c[:, :wide], c[:, wide:]
        filtered = jnp.concatenate([cr * g0 - ci * g1, cr * g1 + ci * g0], axis=1).astype(bf16)
        to_order(m, dot(table[1, m], filtered))
    pack_orders(1)
    start1()
    arrive1()

    start2, arrive2, leave2 = all_to_all(2)
    gain_row = gain[...]
    gain_sum = jnp.zeros_like(gain_row)
    parts = []
    for j in range(rows):
        at = pl.ds(j * lon, lon)
        back = dot(inv_kn[...], unpack_grid(1, j))
        s = (field[at, :].astype(jnp.float32) + back).astype(bf16)
        summed[at, :] = s
        s = s.astype(jnp.float32)
        centered = s - jnp.mean(s, axis=-1, keepdims=True)
        inverse_std = lax.rsqrt(jnp.mean(centered * centered, axis=-1, keepdims=True) + EPSILON)
        normal = centered * inverse_std
        nb = (normal * gain_row).astype(bf16)
        normed[at, :] = nb
        pre = dot(nb, w_in[...])
        phi = 0.5 * (1.0 + lax.erf(pre * 0.7071067811865476))
        hidden[at, :] = (pre * phi).astype(bf16)
        slope = phi + pre * jnp.exp(-0.5 * pre * pre) * 0.3989422804014327
        gp = (up[at, :] * slope).astype(bf16)
        grad_pre[at, :] = gp
        gn = dot_nt(gp, w_in[...])
        gain_sum = gain_sum + jnp.sum(gn * normal, axis=0, keepdims=True)
        v = gn * gain_row
        gs = cot[at, :].astype(jnp.float32) + inverse_std * (
            v
            - jnp.mean(v, axis=-1, keepdims=True)
            - normal * jnp.mean(v * normal, axis=-1, keepdims=True)
        )
        grad_sum[at, :] = gs
        parts.append(dot(inv_nk[...], gs.astype(bf16)))
    pack_grid(2, parts)
    start2()

    mid = w_in.shape[0] // n
    gi = dot_tn(normed[...], grad_pre[...]).astype(bf16)
    wsend[:, :, :mid, :] = gi.reshape(2, chips, mid, gi.shape[1])
    go = dot_tn(hidden[...], cot[...]).astype(bf16).reshape(2, chips, 2 * mid, w_out.shape[1])
    wsend[:, :, mid:, :] = jnp.concatenate([go[:, :, :mid], go[:, :, mid:]], axis=3)

    def pair_copy(slot, source, target):
        return pltpu.make_async_remote_copy(
            src_ref=source, dst_ref=target,
            send_sem=pair_send.at[slot], recv_sem=pair_recv.at[slot],
            device_id=(ens, partner), device_id_type=MESH,
        )

    def chip_exchange(phase, source, target):
        def copy(k):
            to = lax.rem(chip + k, chips)
            return pltpu.make_async_remote_copy(
                src_ref=source(to), dst_ref=target(chip),
                send_sem=chip_send.at[phase, k], recv_sem=chip_recv.at[phase, k],
                device_id=(ens, 2 * to + core), device_id_type=MESH,
            )

        def landing(k):
            origin = lax.rem(chip + chips - k, chips)
            return pltpu.make_async_remote_copy(
                src_ref=source(origin), dst_ref=target(origin),
                send_sem=chip_send.at[phase, k], recv_sem=chip_recv.at[phase, k],
                device_id=(ens, 2 * origin + core), device_id_type=MESH,
            )

        def start(k, _):
            copy(k).start()
            return 0

        def arrive(k, _):
            landing(k).wait_recv()
            return 0

        def leave(k, _):
            copy(k).wait_send()
            return 0

        return (
            lambda: lax.fori_loop(1, chips, start, 0),
            lambda: lax.fori_loop(1, chips, arrive, 0),
            lambda: lax.fori_loop(1, chips, leave, 0),
        )

    pair0 = pair_copy(0, wsend.at[1 - core], wpair)
    pair0.start()
    pair0.wait_recv()
    scatter_start, scatter_arrive, scatter_leave = chip_exchange(
        0, lambda i: wchips.at[i], lambda i: wrecv.at[i]
    )
    wchips[...] = (wsend[core].astype(jnp.float32) + wpair[...].astype(jnp.float32)).astype(bf16)
    wrecv[chip] = wchips[chip]
    scatter_start()

    arrive2()
    start3, arrive3, leave3 = all_to_all(3)
    unpack_orders(2)
    fr = jnp.zeros((degrees, wide), jnp.float32)
    fi = jnp.zeros((degrees, wide), jnp.float32)
    for m in range(rows):
        g = dot(table[2, m], of_order(m))
        gr, gi = g[:, :wide], g[:, wide:]
        c = coeffs[m].astype(jnp.float32)
        cr, ci = c[:, :wide], c[:, wide:]
        fr = fr + (cr * gr + ci * gi)
        fi = fi + (cr * gi - ci * gr)
        gc = jnp.concatenate([gr * g0 + gi * g1, gi * g0 - gr * g1], axis=1).astype(bf16)
        to_order(m, dot(table[3, m], gc))
    pack_orders(3)
    start3()

    for r, f in enumerate((fr, fi)):
        for h in (0, 1):
            nat[2 * r + h] = f[:, h * HALF : (h + 1) * HALF]
    for h, f in enumerate((f0, f1)):
        for r in (0, 1):
            for m in range(rows):
                f[pl.ds(r * rows + m, n, stride=SLOT), :] = nat[
                    2 * r + h, pl.ds(m, n, stride=rows), :
                ]
        f[pl.ds(2 * rows, n, stride=SLOT), :] = jnp.broadcast_to(
            gain_sum[:, h * HALF : (h + 1) * HALF], (n, HALF)
        )
    fsend[...] = jnp.concatenate(
        [f[...].reshape(n, SLOT, HALF) for f in (f0, f1)], axis=1
    ).astype(bf16)
    frecv[me] = fsend[me]
    start4, arrive4, leave4 = exchange(4, lambda i: fsend.at[i], lambda i: frecv.at[i])
    start4()

    gather_start, gather_arrive, gather_leave = chip_exchange(
        1, lambda i: wgather.at[core, chip], lambda i: wgather.at[core, i]
    )
    scatter_arrive()
    wgather[core, chip] = jnp.sum(wrecv[...].astype(jnp.float32), axis=0).astype(bf16)
    gather_start()
    for j in range(rows):
        at = pl.ds(j * lon, lon)
        block_out[at, :] = (
            summed[at, :].astype(jnp.float32) + dot(hidden[at, :], w_out[...])
        ).astype(bf16)
    stores[0].start()

    arrive4()
    ftotal = jnp.sum(frecv[...].astype(jnp.float32), axis=0)
    grad_gain[...] = scale * jnp.concatenate(
        [ftotal[2 * rows : 2 * rows + 1], ftotal[SLOT + 2 * rows : SLOT + 2 * rows + 1]], axis=1
    )
    stores[3].start()
    fgather[me] = ftotal.astype(bf16)
    start5, arrive5, leave5 = exchange(5, lambda i: fgather.at[me], lambda i: fgather.at[i])
    start5()

    arrive3()
    for j in range(rows):
        at = pl.ds(j * lon, lon)
        grad_field[at, :] = (grad_sum[at, :] + dot(fwd_kn[...], unpack_grid(3, j))).astype(bf16)

    stores[1].start()

    gather_arrive()
    pair1 = pair_copy(1, wgather.at[core], wgather.at[core])
    pair1_in = pair_copy(1, wgather.at[1 - core], wgather.at[1 - core])
    pair1.start()

    arrive5()
    fall = fgather[...].astype(jnp.float32) * scale
    f0[...] = fall[:, :SLOT].reshape(n * SLOT, HALF)
    f1[...] = fall[:, SLOT:].reshape(n * SLOT, HALF)
    for h, f in enumerate((f0, f1)):
        for r in (0, 1):
            for m in range(rows):
                nat[2 * r + h, pl.ds(m, n, stride=rows), :] = f[
                    pl.ds(r * rows + m, n, stride=SLOT), :
                ]
            grad_filters[r, :, h * HALF : (h + 1) * HALF] = nat[2 * r + h]

    stores[2].start()
    pair1_in.wait_recv()
    stores[4].start()
    for leave in (leave0, leave1, leave2, leave3, leave4, leave5, scatter_leave, gather_leave):
        leave()
    pair0.wait_send()
    pair1.wait_send()
    for store in stores:
        store.wait()


def write_kernel(scale, *refs):
    count = 5
    sources, refs = refs[:count], refs[count:]
    targets, refs = refs[: count + 1], refs[count + 1 :]
    held, (grad_w_in, grad_w_out, in_sem, out_sem) = refs[:count], refs[count:]
    wgather = held[-1]
    loads = [
        pltpu.make_async_copy(sources[i], held[i], in_sem.at[i]) for i in range(count)
    ]
    stores = [
        pltpu.make_async_copy(source, targets[i], out_sem.at[i])
        for i, source in enumerate((*held[:-1], grad_w_in, grad_w_out))
    ]
    for load in reversed(loads):
        load.start()
    loads[-1].wait()
    _, chips, double, full = wgather.shape
    mid = double // 2
    for c in (0, 1):
        grad_w_in[pl.ds(c * chips * mid, chips * mid), :] = (
            wgather[c, :, :mid, :].astype(jnp.float32) * scale
        ).reshape(chips * mid, full)
        both = wgather[c, :, mid:, :].astype(jnp.float32) * scale
        grad_w_out[pl.ds(2 * c * chips * mid, 2 * chips * mid), :] = jnp.concatenate(
            [both[:, :, : full // 2], both[:, :, full // 2 :]], axis=1
        ).reshape(2 * chips * mid, full // 2)
    stores[-1].start()
    stores[-2].start()
    for i in range(count - 1):
        loads[i].wait()
        stores[i].start()
    for store in stores:
        store.wait()


def legendre_constants(total):
    theta = (np.arange(total) + 0.5) * (math.pi / total)
    x, sine = np.cos(theta), np.sin(theta)
    p = np.zeros((total, total, total), np.float64)
    for m in range(total):
        log_start = 0.5 * (
            math.log((2.0 * m + 1.0) / (4.0 * math.pi))
            + math.lgamma(m + 0.5)
            - math.lgamma(m + 1.0)
            - 0.5 * math.log(math.pi)
        )
        p[:, m, m] = np.exp(log_start + m * np.log(sine))
        if m + 1 < total:
            p[:, m, m + 1] = math.sqrt(2.0 * m + 3.0) * x * p[:, m, m]
        for l in range(m + 2, total):
            a = math.sqrt((4.0 * l * l - 1.0) / (l * l - m * m))
            b = math.sqrt(((l - 1.0) ** 2 - m * m) / (4.0 * (l - 1.0) ** 2 - 1.0))
            p[:, m, l] = a * (x * p[:, m, l - 1] - b * p[:, m, l - 2])
    weights = sine * (math.pi / total)
    return p, weights[:, None, None] * p


def slot_rows(table, n, rows):
    lon = table.shape[2]
    spread = np.zeros((n, SLOT, lon), np.float64)
    spread[:, : 2 * rows] = (
        table.reshape(2, n, rows, lon).transpose(1, 0, 2, 3).reshape(n, 2 * rows, lon)
    )
    return spread.reshape(n * SLOT, lon)


def fused_constants(n, rows, lon):
    total = n * rows
    synth, analysis = legendre_constants(total)
    by_owner = lambda t, axes: t.transpose(axes).reshape(n, rows, total, total)
    tables = np.stack(
        [
            by_owner(analysis, (1, 2, 0)),
            by_owner(synth, (1, 0, 2)),
            by_owner(synth, (1, 2, 0)),
            by_owner(analysis, (1, 0, 2)),
        ],
        axis=1,
    )
    angle = (np.arange(total)[:, None] * np.arange(lon)[None, :] % lon) * (2.0 * math.pi / lon)
    wave = np.stack([np.cos(angle), -np.sin(angle)])
    forward = slot_rows(wave * (2.0 * math.pi / lon), n, rows)
    inverse = slot_rows(wave * np.where(np.arange(total) == 0, 1.0, 2.0)[:, None], n, rows)
    cast = lambda t: np.asarray(t, np.float32).astype(ml_dtypes.bfloat16)
    return (
        cast(forward), cast(inverse.T), cast(inverse), cast(forward.T), cast(tables),
    )


def fused(field, filters, weight_in, weight_out, norm_gain, cotangent):
    n = lax.axis_size("lat")
    _, rows, lon, channels = field.shape
    hid = weight_in.shape[1]
    cells, total, chips = rows * lon, rows * n, n // 2
    mid = channels // n
    f32, bf16 = jnp.float32, jnp.bfloat16
    scale = 1.0 / math.sqrt(total * lon)
    constants = fused_constants(n, rows, lon)
    hbm = pl.BlockSpec(memory_space=pltpu.HBM)
    phases = 4
    outs = pl.pallas_call(
        functools.partial(fused_kernel, n, rows, lon, scale),
        out_shape=(
            jax.ShapeDtypeStruct((cells, channels), bf16),
            jax.ShapeDtypeStruct((cells, channels), bf16),
            jax.ShapeDtypeStruct((2, total, channels), f32),
            jax.ShapeDtypeStruct((1, channels), f32),
            jax.ShapeDtypeStruct((2, chips, 2 * mid, hid), bf16),
        ),
        in_specs=[hbm] * 11,
        out_specs=(hbm,) * 5,
        scratch_shapes=[
            pltpu.VMEM((phases, n, 2 * rows * SLOT, HALF), bf16),
            pltpu.VMEM((phases, n, 2 * rows * SLOT, HALF), bf16),
            pltpu.VMEM((n, 2 * SLOT, HALF), bf16),
            pltpu.VMEM((n, 2 * SLOT, HALF), bf16),
            pltpu.VMEM((n, 2 * SLOT, HALF), bf16),
            pltpu.VMEM((2, chips, 2 * mid, hid), bf16),
            pltpu.VMEM((chips, 2 * mid, hid), bf16),
            pltpu.VMEM((chips, 2 * mid, hid), bf16),
            pltpu.VMEM((chips, 2 * mid, hid), bf16),
            pltpu.VMEM((2, chips, 2 * mid, hid), bf16),
            pltpu.VMEM((4, rows, total, total), bf16),
            pltpu.VMEM((cells, hid), f32),
            pltpu.VMEM((cells, channels), bf16),
            pltpu.VMEM((cells, channels), bf16),
            pltpu.VMEM((cells, hid), bf16),
            pltpu.VMEM((cells, hid), bf16),
            pltpu.VMEM((cells, channels), f32),
            pltpu.VMEM((rows, total, 2 * channels), bf16),
            pltpu.VMEM((total * SLOT, HALF), f32),
            pltpu.VMEM((total * SLOT, HALF), f32),
            pltpu.VMEM((total * SLOT, HALF), f32),
            pltpu.VMEM((total * SLOT, HALF), f32),
            pltpu.VMEM((n * SLOT, HALF), f32),
            pltpu.VMEM((n * SLOT, HALF), f32),
            pltpu.VMEM((4, total, HALF), f32),
            pltpu.VMEM((cells, channels), bf16),
            pltpu.VMEM(filters.shape, bf16),
            pltpu.VMEM(weight_in.shape, bf16),
            pltpu.VMEM(weight_out.shape, bf16),
            pltpu.VMEM((1, channels), f32),
            pltpu.VMEM((cells, channels), bf16),
            *[pltpu.VMEM(t.shape, bf16) for t in constants[:4]],
            pltpu.VMEM((cells, channels), bf16),
            pltpu.VMEM((cells, channels), bf16),
            pltpu.VMEM((2, total, channels), f32),
            pltpu.VMEM((1, channels), f32),
            pltpu.SemaphoreType.DMA((6, n)),
            pltpu.SemaphoreType.DMA((6, n)),
            pltpu.SemaphoreType.DMA((2, chips)),
            pltpu.SemaphoreType.DMA((2, chips)),
            pltpu.SemaphoreType.DMA((2,)),
            pltpu.SemaphoreType.DMA((2,)),
            pltpu.SemaphoreType.DMA((11,)),
            pltpu.SemaphoreType.DMA((5,)),
        ],
        compiler_params=pltpu.CompilerParams(
            collective_id=0, has_side_effects=True, vmem_limit_bytes=VMEM_LIMIT
        ),
    )(
        field.reshape(cells, channels), filters, weight_in, weight_out,
        norm_gain.reshape(1, channels), cotangent.reshape(cells, channels),
        *[jnp.asarray(t) for t in constants],
    )
    weight_shapes = ((channels, hid), (hid, channels))
    outs = pl.pallas_call(
        functools.partial(write_kernel, scale),
        out_shape=(
            *[jax.ShapeDtypeStruct(o.shape, o.dtype) for o in outs[:-1]],
            *[jax.ShapeDtypeStruct(shape, f32) for shape in weight_shapes],
        ),
        in_specs=[hbm] * 5,
        out_specs=(hbm,) * 6,
        scratch_shapes=[
            *[pltpu.VMEM(o.shape, o.dtype) for o in outs],
            *[pltpu.VMEM(shape, f32) for shape in weight_shapes],
            pltpu.SemaphoreType.DMA((5,)),
            pltpu.SemaphoreType.DMA((6,)),
        ],
        compiler_params=pltpu.CompilerParams(vmem_limit_bytes=VMEM_LIMIT),
    )(*outs)
    return (
        outs[0].reshape(field.shape), outs[1].reshape(field.shape),
        outs[2], outs[4], outs[5], outs[3].reshape(channels),
    )


def block(field, filters, weight_in, weight_out, norm_gain, cotangent):
    n = lax.axis_size("lat")
    members, rows, lon, channels = field.shape
    hid = weight_in.shape[1]
    fits = (
        members == 1
        and n % 2 == 0
        and 2 * rows < SLOT
        and channels == 2 * HALF
        and hid == 2 * channels
        and channels % (TILE * n) == 0
        and (rows * n) % TILE == 0
        and lon % TILE == 0
        and rows * lon * hid <= 512 * 1024
    )
    chosen = fused if fits else shards
    return chosen(field, filters, weight_in, weight_out, norm_gain, cotangent)


def solution(mesh):
    placed = (P("ens", "lat", None, None), P(), P(), P(), P(), P("ens", "lat", None, None))
    return jax.shard_map(
        block,
        mesh=mesh,
        in_specs=placed,
        out_specs=(
            P("ens", "lat", None, None),
            P("ens", "lat", None, None),
            P("ens", None, None),
            P("ens", None),
            P("ens", None),
            P("ens"),
        ),
        check_vma=False,
    )
```
